32 devices in a mesh: fsdp: 32 (over z, y, x, core).
Axes of the slice: x: 2, y: 2, z: 4, core: 2. Of those that a mesh axis runs over, the one named last changes fastest.
Arguments:
- tokens: bfloat16 [32768, 1024], P('fsdp'), may hold values from -6 to 6
- lengths: int32 [64], P('fsdp'), may hold values from 128 to 512, as said below
- cotangent: bfloat16 [32768, 1024], P('fsdp'), may hold values from -6 to 6
- query_weight: bfloat16 [1024, 1024], P('fsdp'), may hold values from -0.1875 to 0.1875
- query_bias: bfloat16 [1024], P('fsdp'), may hold values from -3 to 3
- key_weight: bfloat16 [1024, 1024], P('fsdp'), may hold values from -0.1875 to 0.1875
- value_weight: bfloat16 [1024, 1024], P('fsdp'), may hold values from -0.1875 to 0.1875
- value_bias: bfloat16 [1024], P('fsdp'), may hold values from -3 to 3
- attn_weight: bfloat16 [1024, 1024], P('fsdp'), may hold values from -1.5 to 1.5
- attn_bias: bfloat16 [1024], P('fsdp'), may hold values from -3 to 3
- first_gain: bfloat16 [1024], P('fsdp'), may hold values from 0.5 to 1.5
- first_shift: bfloat16 [1024], P('fsdp'), may hold values from -3 to 3
- inner_weight: bfloat16 [1024, 4096], P('fsdp'), may hold values from -0.1875 to 0.1875
- inner_bias: bfloat16 [4096], P('fsdp'), may hold values from -3 to 3
- outer_weight: bfloat16 [4096, 1024], P('fsdp'), may hold values from -0.09375 to 0.09375
- outer_bias: bfloat16 [1024], P('fsdp'), may hold values from -3 to 3
- second_gain: bfloat16 [1024], P('fsdp'), may hold values from 0.5 to 1.5
- second_shift: bfloat16 [1024], P('fsdp'), may hold values from -3 to 3
Outputs:
- output: bfloat16 [32768, 1024], P('fsdp')
- input_grad: bfloat16 [32768, 1024], P('fsdp')
- query_wgrad: float32 [1024, 1024], P('fsdp')
- query_bgrad: float32 [1024], P('fsdp')
- key_wgrad: float32 [1024, 1024], P('fsdp')
- value_wgrad: float32 [1024, 1024], P('fsdp')
- value_bgrad: float32 [1024], P('fsdp')
- attn_wgrad: float32 [1024, 1024], P('fsdp')
- attn_bgrad: float32 [1024], P('fsdp')
- first_ggrad: float32 [1024], P('fsdp')
- first_sgrad: float32 [1024], P('fsdp')
- inner_wgrad: float32 [1024, 4096], P('fsdp')
- inner_bgrad: float32 [4096], P('fsdp')
- outer_wgrad: float32 [4096, 1024], P('fsdp')
- outer_bgrad: float32 [1024], P('fsdp')
- second_ggrad: float32 [1024], P('fsdp')
- second_sgrad: float32 [1024], P('fsdp')
The draws below stay inside these ranges and needn't reach their ends.
Inputs may be any that keep to these rules, and one draw needn't show every extreme that they name: The first lengths[s] slots of sequence s are valid; some sequence has exactly 512 valid slots and some has exactly 128.
All inputs are finite; a program needn't handle non-finite values.
Results may differ from the reference program's by a relative error of at most 0.014.
Values may be sent and summed in bfloat16 or wider, within the bound.
No kernel may reach another device: no remote copies, remote signals or barrier semaphores. Data moves between devices by JAX's collectives and lax.ppermute only.
A program may use at most 256 MiB of HBM per device.

```python
import math
import jax
import jax.numpy as jnp
from jax import lax

D = 1024
HEADS = 16
DHEAD = 64
FF = 4096
LEN = 512
MIN_LEN = 128
SEQS = 64
TOKENS = 32768


def draw_lengths(key, part):
    key = jax.random.fold_in(key, 7)
    first_key, second_key = jax.random.split(key)
    base = jax.random.randint(first_key, (SEQS,), MIN_LEN, LEN + 1)
    order = jax.random.permutation(second_key, SEQS)
    base = base.at[order[0]].set(LEN)
    base = base.at[order[1]].set(MIN_LEN)
    return base.astype(jnp.int32)


def strengthened(entries, rng, source, target, shards_of, factor):
    owner, partner = [(jnp.arange(entries.shape[position]) // (entries.shape[position] // shards_of)).reshape([-1 if axis == position else 1 for axis in range(entries.ndim)]) for position in (source, target)]
    chosen = jax.random.permutation(rng, shards_of)[partner]
    strong = (owner == chosen) | (owner == (partner + shards_of // 2) % shards_of)
    return jnp.where(strong, factor * entries, entries)


def level_of(own_key, shape, cuts, smallest, largest):
    level = 1.0
    for position, blocks in cuts:
        draws = jax.random.uniform(jax.random.fold_in(jax.random.fold_in(own_key, 6), position), (blocks,), jnp.float32, smallest / len(cuts), largest / len(cuts))
        level = level * jnp.repeat(jnp.exp(draws), shape[position] // blocks).reshape((-1,) + (1,) * (len(shape) - 1 - position))
    return level


def scatter_about(key, shape, width, limit, cuts=(), dtype=jnp.bfloat16):
    drawn = width * jax.random.normal(key, shape, jnp.float32)
    if cuts:
        drawn = drawn * level_of(key, shape, cuts, -0.22, 0.18)
    return jnp.clip(drawn, -limit, limit).astype(dtype)


def gaussian_with(rng, shape, width, most, pieces, heavy, held_as=jnp.bfloat16):
    entries = width * jax.random.normal(rng, shape, jnp.float32)
    if pieces:
        entries = entries * level_of(rng, shape, pieces, -0.22, 0.18)
    return jnp.clip(strengthened(entries, jax.random.fold_in(rng, 3), *heavy), -most, most).astype(held_as)


def setup_inputs(seed: int = 0) -> dict:
    key_of = jax.random.split(jax.random.key(seed), 19)
    tokens = scatter_about(key_of[0], (TOKENS, D), 1.0, 6.0, ((0, 32),))
    lengths = draw_lengths(jax.random.fold_in(key_of[18], 71), 0)
    cotangent = gaussian_with(key_of[2], (TOKENS, D), 1.0, 6.0, ((0, 32),), (0, 1, 32, 2.75))
    query_weight = scatter_about(key_of[3], (D, D), D ** -0.5, 0.1875, ((0, 32),))
    query_bias = scatter_about(key_of[4], (D,), 0.5, 3.0, ((0, 32),))
    key_weight = scatter_about(key_of[5], (D, D), D ** -0.5, 0.1875, ((0, 32),))
    value_weight = scatter_about(key_of[6], (D, D), D ** -0.5, 0.1875, ((0, 32),))
    value_bias = scatter_about(key_of[7], (D,), 0.5, 3.0, ((0, 32),))
    attn_weight = scatter_about(key_of[8], (D, D), (D // 64) ** -0.5, 1.5, ((0, 32),))
    attn_bias = scatter_about(key_of[9], (D,), 0.5, 3.0, ((0, 32),))
    first_gain = jnp.clip(1.0 + 0.1 * jax.random.normal(key_of[10], (D,), jnp.float32), 0.5, 1.5).astype(jnp.bfloat16)
    first_shift = scatter_about(key_of[11], (D,), 0.5, 3.0, ((0, 32),))
    inner_weight = scatter_about(key_of[12], (D, FF), D ** -0.5, 0.1875, ((0, 32),))
    inner_bias = scatter_about(key_of[13], (FF,), 0.5, 3.0, ((0, 32),))
    outer_weight = scatter_about(key_of[14], (FF, D), FF ** -0.5, 0.09375, ((0, 32),))
    outer_bias = scatter_about(key_of[15], (D,), 0.5, 3.0, ((0, 32),))
    second_gain = jnp.clip(1.0 + 0.1 * jax.random.normal(key_of[16], (D,), jnp.float32), 0.5, 1.5).astype(jnp.bfloat16)
    second_shift = scatter_about(key_of[17], (D,), 0.5, 3.0, ((0, 32),))
    return dict(tokens=tokens, lengths=lengths, cotangent=cotangent, query_weight=query_weight, query_bias=query_bias, key_weight=key_weight, value_weight=value_weight, value_bias=value_bias, attn_weight=attn_weight, attn_bias=attn_bias, first_gain=first_gain, first_shift=first_shift, inner_weight=inner_weight, inner_bias=inner_bias, outer_weight=outer_weight, outer_bias=outer_bias, second_gain=second_gain, second_shift=second_shift)


@jax.custom_vjp
def low(v):
    return lax.optimization_barrier(v.astype(jnp.bfloat16)).astype(jnp.float32)

@jax.custom_vjp
def low_back(v):
    return v

def low_keep(v):
    return (low(v), None)

def low_pass(kept, grad):
    return (grad,)

def back_keep(v):
    return (v, None)

def back_low(kept, grad):
    return (low(grad),)
low.defvjp(low_keep, low_pass)
low_back.defvjp(back_keep, back_low)
EPSILON = 1e-05
MASKED = -1e+30

def product(left, right):
    return jnp.dot(left, right, precision=lax.Precision.HIGHEST)

def layer_norm(rows):
    centre = lax.optimization_barrier(jnp.mean(rows, axis=-1, keepdims=True))
    centred = rows - centre
    return centred * lax.rsqrt(lax.optimization_barrier(jnp.mean(centred * centred, axis=-1, keepdims=True)) + EPSILON)

def attend(inputs):
    query, keys, values, length = inputs
    scores = jnp.einsum('qhd,khd->hqk', query, keys, precision=lax.Precision.HIGHEST) * DHEAD ** (-0.5)
    scores = low_back(scores)
    places = lax.broadcasted_iota(jnp.int32, scores.shape, 2)
    scores = jnp.where(places < length, scores, MASKED)
    top = lax.optimization_barrier(jnp.max(scores, axis=-1, keepdims=True))
    expo = jnp.exp(scores - top)
    probs = expo / lax.optimization_barrier(jnp.sum(expo, axis=-1, keepdims=True))
    return jnp.einsum('hqk,khd->qhd', low(probs), values, precision=lax.Precision.HIGHEST)

def forward(params, rows, lens_group):
    query_weight, query_bias, key_weight, value_weight, value_bias, attn_weight, attn_bias, first_gain, first_shift, inner_weight, inner_bias, outer_weight, outer_bias, second_gain, second_shift = params
    count = lens_group.shape[0]
    query = low_back(low(product(rows, query_weight) + query_bias))
    keys = low_back(low(product(rows, key_weight)))
    values = low_back(low(product(rows, value_weight) + value_bias))
    shape = (count, LEN, HEADS, DHEAD)
    mixed = lax.map(jax.checkpoint(attend), (query.reshape(shape), keys.reshape(shape), values.reshape(shape), lens_group))
    mixed = low_back(low(mixed.reshape(count * LEN, D)))
    first_sum = rows + low_back(product(mixed, attn_weight) + attn_bias)
    middle = layer_norm(first_sum) * first_gain + first_shift
    hidden = low_back(product(low(middle), inner_weight) + inner_bias)
    active = low(jax.nn.gelu(hidden, approximate=False))
    second_sum = middle + low_back(product(active, outer_weight) + outer_bias)
    return layer_norm(second_sum) * second_gain + second_shift

def reference(tokens, lengths, cotangent, query_weight, query_bias, key_weight, value_weight, value_bias, attn_weight, attn_bias, first_gain, first_shift, inner_weight, inner_bias, outer_weight, outer_bias, second_gain, second_shift):
    params = tuple((p.astype(jnp.float32) for p in (query_weight, query_bias, key_weight, value_weight, value_bias, attn_weight, attn_bias, first_gain, first_shift, inner_weight, inner_bias, outer_weight, outer_bias, second_gain, second_shift)))
    per = math.gcd(SEQS, max(1, 4096 // LEN))
    groups = SEQS // per
    places = lax.broadcasted_iota(jnp.int32, (SEQS, LEN), 1)
    valid = (places < lengths[:, None]).astype(jnp.float32).reshape(TOKENS, 1)
    grad_rows = cotangent.astype(jnp.float32) * valid
    rows_all = tokens.astype(jnp.float32).reshape(groups, per * LEN, D)
    lens_all = lengths.reshape(groups, per)
    cot_all = grad_rows.reshape(groups, per * LEN, D)

    def step(totals, inputs):
        rows, lens_group, cot_group = inputs
        result, pull = jax.vjp(lambda pr, xr: forward(pr, xr, lens_group), params, rows)
        grad_params, grad_input = pull(cot_group)
        totals = jax.tree.map(lambda a, b: a + b, totals, grad_params)
        return (totals, (result.astype(jnp.bfloat16), grad_input.astype(jnp.bfloat16)))
    start = jax.tree.map(lambda p: jnp.zeros(p.shape, jnp.float32), params)
    totals, (results, inputs_back) = lax.scan(step, start, (rows_all, lens_all, cot_all))
    output = results.reshape(TOKENS, D)
    input_grad = inputs_back.reshape(TOKENS, D)
    return (output, input_grad, totals[0], totals[1], totals[2], totals[3], totals[4], totals[5], totals[6], totals[7], totals[8], totals[9], totals[10], totals[11], totals[12], totals[13], totals[14])
```

```python
from functools import partial

import jax
import jax.numpy as jnp
from jax import lax
from jax.experimental import pallas as pl
from jax.experimental.pallas import tpu as pltpu
from jax.sharding import PartitionSpec as P

HEADS = 16
DHEAD = 64
EPSILON = 1e-05
MASKED = -1e30
SCALE = DHEAD ** (-0.5)
F32 = jnp.float32
BF16 = jnp.bfloat16
BLOCK = 256
VMEM_LIMIT = 60 * 1024 * 1024
SIDES = (0, 2, 4, 6)


def dot(left, right):
    return jnp.dot(left, right, preferred_element_type=F32)


def dot_nt(left, right):
    return lax.dot_general(left, right, (((1,), (1,)), ((), ())), preferred_element_type=F32)


def dot_tn(left, right):
    return lax.dot_general(left, right, (((0,), (0,)), ((), ())), preferred_element_type=F32)


def normalize(rows):
    centred = rows - jnp.mean(rows, axis=-1, keepdims=True)
    factor = lax.rsqrt(jnp.mean(centred * centred, axis=-1, keepdims=True) + EPSILON)
    return centred * factor, factor


def norm_back(grad, normed, factor):
    mean_one = jnp.mean(grad, axis=-1, keepdims=True)
    mean_two = jnp.mean(grad * normed, axis=-1, keepdims=True)
    return factor * (grad - mean_one - normed * mean_two)


def flip(array, bits):
    n = lax.axis_size("fsdp")
    return lax.ppermute(array, "fsdp", [(i, i ^ bits) for i in range(n)])


def after(array, others):
    return lax.optimization_barrier((array,) + tuple(others))[0]


class Weight:
    def __init__(self, pieces, slot, offset, count, rows, columns):
        self.pieces, self.slot, self.offset, self.count = pieces, slot, offset, count
        self.rows, self.columns = rows, columns


def gather_pieces(shard, through):
    n = lax.axis_size("fsdp")
    others = [flip(shard, 8 * k) for k in range(1, n // 8)]
    line = jnp.concatenate([shard] + others) if others else shard
    beside, above = flip(line, 2), flip(line, 4)
    across = flip(above, 2) if through == 2 else flip(beside, 4)
    near = (line, beside, above, across)
    return near + tuple(flip(piece, 1) for piece in near), others


def start_load(weight, refs, target, here, sem, columns=None):
    column = slice(None) if columns is None else columns
    if len(refs) == 1:
        pltpu.make_async_copy(refs[0].at[:, column], target, sem).start()
        return
    count = weight.count
    places = weight.rows // count // 8
    for low, ref in zip(SIDES + tuple(s ^ 1 for s in SIDES), refs):
        for k in range(places):
            owner = here ^ (low ^ (8 * k))
            pltpu.make_async_copy(
                ref.at[pl.ds(k * weight.slot + weight.offset, count), column],
                target.at[pl.ds(pl.multiple_of(owner * count, count), count)],
                sem,
            ).start()


def wait_load(target, sem):
    pltpu.make_async_copy(target, target, sem).wait()


def sum_everywhere(array):
    n = lax.axis_size("fsdp")
    bit = 1
    while bit < n:
        array = array + flip(array, bit)
        bit *= 2
    return array


def add_low(*arrays):
    total = arrays[0].astype(F32)
    for array in arrays[1:]:
        total = total + array.astype(F32)
    return total


def scatter_pieces(keep, send, through):
    low = lambda *arrays: add_low(*arrays).astype(BF16)
    got = flip(send, 1)
    across = low(keep[3], got[3])
    beside, above = None, None
    if through == 2:
        moved = flip(across, 2)
        above = low(keep[2], got[2], moved)
        beside = low(keep[1], got[1])
    else:
        moved = flip(across, 4)
        beside = low(keep[1], got[1], moved)
        above = low(keep[2], got[2])
    from_beside = flip(beside, 2)
    from_above = flip(above, 4)
    places = keep.shape[1]
    pieces = [
        add_low(keep[0, k], got[0, k], from_beside[k], from_above[k]) for k in range(places)
    ]
    arrived = [flip(pieces[k].astype(BF16), 8 * k) for k in range(1, places)]
    return add_low(pieces[0], *arrived)


def operands_of(weights):
    arrays, where = [], []
    for weight in weights:
        places = []
        for piece in weight.pieces:
            for position, array in enumerate(arrays):
                if array is piece:
                    places.append(position)
                    break
            else:
                places.append(len(arrays))
                arrays.append(piece)
        where.append(places)
    return arrays, where


def call(body, grid, info, inputs, specs, weights, outs, out_specs, scratch, flops, name, exps=0):
    arrays, where = operands_of(weights)
    count = len(inputs)

    def kernel(info_ref, *refs):
        ins = refs[:count]
        pieces = refs[count : count + len(arrays)]
        held = [[pieces[p] for p in places] for places in where]
        body(info_ref, ins, held, refs[count + len(arrays) :])

    moved = sum(a.size * a.dtype.itemsize for a in list(inputs) + arrays)
    moved += sum(o.size * o.dtype.itemsize for o in jax.tree.leaves(outs))
    return pl.pallas_call(
        kernel,
        grid_spec=pltpu.PrefetchScalarGridSpec(
            num_scalar_prefetch=1,
            grid=grid,
            in_specs=list(specs) + [pl.BlockSpec(memory_space=pl.ANY)] * len(arrays),
            out_specs=out_specs,
            scratch_shapes=scratch,
        ),
        out_shape=outs,
        compiler_params=pltpu.CompilerParams(
            vmem_limit_bytes=VMEM_LIMIT, dimension_semantics=("arbitrary",) * len(grid)
        ),
        cost_estimate=pl.CostEstimate(flops=flops, bytes_accessed=moved, transcendentals=exps),
        name=name,
    )(info, *inputs, *arrays)


def shape_of(shape, dtype):
    return jax.ShapeDtypeStruct(shape, dtype)


def whole(shape):
    return pl.BlockSpec(shape, lambda *_: (0,) * len(shape))


def by_rows(columns, rows=BLOCK):
    return pl.BlockSpec((rows, columns), lambda i, *_: (i, 0))


def project_qkv(info, tokens, biases, weights):
    rows, width = tokens.shape

    def body(info_ref, ins, held, rest):
        tokens_ref, bias_ref = ins
        out_ref, matrix, sem = rest
        which = pl.program_id(0)

        @pl.when(which == 0)
        def _():
            for i, weight in enumerate(weights):
                start_load(weight, held[i], matrix.at[i], info_ref[0], sem.at[i])

        wait_load(matrix.at[which], sem.at[which])
        factor = jnp.where(which == 0, SCALE, 1.0).astype(F32)
        for start in range(0, rows, BLOCK):
            part = pl.ds(start, BLOCK)
            total = dot(tokens_ref[part, :], matrix[which]) + bias_ref[0]
            out_ref[0, part, :] = (total * factor).astype(BF16)

    return call(
        body,
        (3,),
        info,
        (tokens, biases),
        (whole(tokens.shape), pl.BlockSpec((1, 1, width), lambda i, *_: (i, 0, 0))),
        weights,
        shape_of((3, rows, width), BF16),
        pl.BlockSpec((1, rows, width), lambda i, *_: (i, 0, 0)),
        [pltpu.VMEM((3, width, width), BF16), pltpu.SemaphoreType.DMA((3,))],
        6 * rows * width * width,
        "project_qkv",
    )


def head_masks(span, length):
    lane = lax.broadcasted_iota(jnp.int32, (span, 2 * DHEAD), 1)
    place = lax.broadcasted_iota(jnp.int32, (span, 2 * DHEAD), 0)
    return lane, jnp.where(place < length, 0.0, MASKED).astype(F32)


def marked(array, lane, head, mark):
    own = lane // DHEAD == head
    spare = lane == (1 - head) * DHEAD
    return jnp.where(own, array.astype(F32), jnp.where(spare, mark, 0.0)).astype(BF16)


def attend(info, qkv, seqs):
    _, rows, width = qkv.shape
    span = rows // seqs
    pairs = width // (2 * DHEAD)

    def body(info_ref, ins, held, rest):
        query_ref, key_ref, value_ref = ins
        mixed_ref, logsum_ref = rest
        length = info_ref[1 + pl.program_id(0)]
        lane, mark = head_masks(span, length)
        query, keys = query_ref[0], key_ref[0]
        value_t = value_ref[0].T
        mixed = []
        for head in range(2):
            key_one = marked(keys, lane, head, mark)
            query_one = marked(query, lane, head, 1.0)
            scores = dot_nt(key_one, query_one)
            top = jnp.max(scores, axis=0, keepdims=True)
            expo = jnp.exp(scores - top)
            total = jnp.sum(expo, axis=0, keepdims=True)
            out = dot(value_t[head * DHEAD : (head + 1) * DHEAD], expo.astype(BF16))
            mixed.append(out / total)
            logsum_ref[0, 0, head : head + 1, :] = top + jnp.log(total)
        mixed_ref[...] = jnp.concatenate(mixed, axis=0).T.astype(BF16)

    def block(which):
        return pl.BlockSpec((1, span, 2 * DHEAD), lambda s, p, *_: (which, s, p))

    return call(
        body,
        (seqs, pairs),
        info,
        (qkv, qkv, qkv),
        [block(i) for i in range(3)],
        [],
        (shape_of((rows, width), BF16), shape_of((seqs, pairs, 8, span), F32)),
        (
            pl.BlockSpec((span, 2 * DHEAD), lambda s, p, *_: (s, p)),
            pl.BlockSpec((1, 1, 8, span), lambda s, p, *_: (s, p, 0, 0)),
        ),
        [],
        8 * rows * span * width,
        "attend",
        exps=rows * span * HEADS,
    )


def attend_back(info, qkv, grad_mixed, logsum, seqs):
    _, rows, width = qkv.shape
    span = rows // seqs
    pairs = width // (2 * DHEAD)

    def body(info_ref, ins, held, rest):
        query_ref, key_ref, value_ref, grad_ref, logsum_ref = ins
        step_ref, sums_ref = rest
        length = info_ref[1 + pl.program_id(0)]
        lane, mark = head_masks(span, length)
        query, keys, values, grad = query_ref[0], key_ref[0], value_ref[0], grad_ref[...]
        key_t = keys.T
        query_steps, key_steps, value_steps = [], [], []
        for head in range(2):
            key_one = marked(keys, lane, head, mark)
            query_one = marked(query, lane, head, 1.0)
            value_one = marked(values, lane, head, 0.0)
            scores = dot_nt(key_one, query_one)
            probs = jnp.exp(scores - logsum_ref[0, 0, head : head + 1, :])
            grad_probs = dot_nt(value_one, grad)
            value_steps.append(dot(probs.astype(BF16), grad))
            inner = jnp.sum(grad_probs * probs, axis=0, keepdims=True)
            grad_scores = (probs * (grad_probs - inner)).astype(BF16)
            key_steps.append(dot(grad_scores, query))
            query_steps.append(
                dot(key_t[head * DHEAD : (head + 1) * DHEAD], grad_scores) * SCALE
            )
        first = lane < DHEAD
        query_step = jnp.concatenate(query_steps, axis=0).T.astype(BF16)
        key_step = jnp.where(first, key_steps[0], key_steps[1]).astype(BF16)
        value_step = jnp.where(first, value_steps[0], value_steps[1]).astype(BF16)
        step_ref[0] = query_step
        step_ref[1] = key_step
        step_ref[2] = value_step
        sums_ref[0, 0:1, :] = jnp.sum(query_step.astype(F32), axis=0, keepdims=True)
        sums_ref[0, 1:2, :] = jnp.sum(value_step.astype(F32), axis=0, keepdims=True)

    def block(which):
        return pl.BlockSpec((1, span, 2 * DHEAD), lambda s, p, *_: (which, s, p))

    return call(
        body,
        (seqs, pairs),
        info,
        (qkv, qkv, qkv, grad_mixed, logsum),
        [block(i) for i in range(3)]
        + [
            pl.BlockSpec((span, 2 * DHEAD), lambda s, p, *_: (s, p)),
            pl.BlockSpec((1, 1, 8, span), lambda s, p, *_: (s, p, 0, 0)),
        ],
        [],
        (shape_of((3, rows, width), BF16), shape_of((seqs, 8, width), F32)),
        (
            pl.BlockSpec((3, span, 2 * DHEAD), lambda s, p, *_: (0, s, p)),
            pl.BlockSpec((1, 8, 2 * DHEAD), lambda s, p, *_: (s, 0, p)),
        ),
        [],
        20 * rows * span * width,
        "attend_back",
        exps=rows * span * HEADS,
    )


def project_out(info, mixed, tokens, vectors, weight):
    rows, width = tokens.shape

    def body(info_ref, ins, held, rest):
        mixed_ref, tokens_ref, vector_ref = ins
        normed_ref, low_ref, factor_ref, matrix, sem = rest

        @pl.when(pl.program_id(0) == 0)
        def _():
            start_load(weight, held[0], matrix, info_ref[0], sem)
            wait_load(matrix, sem)

        branch = dot(mixed_ref[...], matrix[...]) + vector_ref[2:3, :]
        normed, factor = normalize(tokens_ref[...].astype(F32) + branch)
        normed_ref[...] = normed
        low_ref[...] = (normed * vector_ref[3:4, :] + vector_ref[4:5, :]).astype(BF16)
        factor_ref[...] = jnp.broadcast_to(factor, factor_ref.shape)

    return call(
        body,
        (rows // BLOCK,),
        info,
        (mixed, tokens, vectors),
        (by_rows(width), by_rows(width), whole(vectors.shape)),
        [weight],
        (shape_of((rows, width), F32), shape_of((rows, width), BF16), shape_of((rows, 128), F32)),
        (by_rows(width), by_rows(width), by_rows(128)),
        [pltpu.VMEM((width, width), BF16), pltpu.SemaphoreType.DMA],
        2 * rows * width * width,
        "project_out",
    )


def gelu_both(hidden):
    size = jnp.abs(hidden) * 0.7071067811865476
    ratio = 1.0 / (1.0 + 0.3275911 * size)
    bell = jnp.exp(-0.5 * (hidden * hidden))
    series = 0.5 * 1.061405429 * ratio + 0.5 * -1.453152027
    series = series * ratio + 0.5 * 1.421413741
    series = series * ratio + 0.5 * -0.284496736
    series = series * ratio + 0.5 * 0.254829592
    tail = series * ratio * bell
    share = jnp.where(hidden >= 0, 1.0 - tail, tail)
    return hidden * share, share + hidden * bell * 0.3989422804014327


def feed_in(info, low, bias, weight):
    rows, width = low.shape
    wide = weight.columns
    part = min(1024, wide)
    steps = wide // part

    def body(info_ref, ins, held, rest):
        low_ref, bias_ref = ins
        active_ref, slope_ref, matrix, sem = rest
        step = pl.program_id(0)

        @pl.when(step == 0)
        def _():
            for i in range(steps):
                start_load(
                    weight, held[0], matrix.at[i], info_ref[0], sem.at[i], pl.ds(i * part, part)
                )

        wait_load(matrix.at[step], sem.at[step])
        for start in range(0, rows, BLOCK):
            some = pl.ds(start, BLOCK)
            hidden = dot(low_ref[some, :], matrix[step]) + bias_ref[...]
            active, slope = gelu_both(hidden)
            active_ref[some, :] = active.astype(BF16)
            slope_ref[some, :] = slope.astype(BF16)

    columns = pl.BlockSpec((rows, part), lambda i, *_: (0, i))
    return call(
        body,
        (steps,),
        info,
        (low, bias),
        (whole(low.shape), pl.BlockSpec((1, part), lambda i, *_: (0, i))),
        [weight],
        (shape_of((rows, wide), BF16), shape_of((rows, wide), BF16)),
        (columns, columns),
        [pltpu.VMEM((steps, width, part), BF16), pltpu.SemaphoreType.DMA((steps,))],
        2 * rows * width * wide,
        "feed_in",
        exps=rows * wide,
    )


def feed_out(info, active, normed, cotangent, vectors, weight, span):
    rows, wide = active.shape
    width = weight.columns

    def body(info_ref, ins, held, rest):
        active_ref, normed_ref, cotangent_ref, vector_ref = ins
        out_ref, second_ref, sums_ref, matrix, sem = rest
        step = pl.program_id(0)

        @pl.when(step == 0)
        def _():
            start_load(weight, held[0], matrix, info_ref[0], sem)
            sums_ref[...] = jnp.zeros_like(sums_ref)
            wait_load(matrix, sem)

        middle = normed_ref[...] * vector_ref[3:4, :] + vector_ref[4:5, :]
        branch = dot(active_ref[...], matrix[...]) + vector_ref[5:6, :]
        second, factor = normalize(middle + branch)
        gain = vector_ref[6:7, :]
        out_ref[...] = (second * gain + vector_ref[7:8, :]).astype(BF16)
        places = step * BLOCK + lax.broadcasted_iota(jnp.int32, (BLOCK, 1), 0)
        sequence = (step * BLOCK) // span
        length = info_ref[1 + sequence]
        valid = places - sequence * span < length
        grad = jnp.where(valid, cotangent_ref[...].astype(F32), 0.0)
        sums_ref[0:1, :] += jnp.sum(grad * second, axis=0, keepdims=True)
        sums_ref[1:2, :] += jnp.sum(grad, axis=0, keepdims=True)
        back = norm_back(grad * gain, second, factor)
        second_ref[...] = back
        sums_ref[2:3, :] += jnp.sum(back.astype(BF16).astype(F32), axis=0, keepdims=True)

    return call(
        body,
        (rows // BLOCK,),
        info,
        (active, normed, cotangent, vectors),
        (by_rows(wide), by_rows(width), by_rows(width), whole(vectors.shape)),
        [weight],
        (
            shape_of((rows, width), BF16),
            shape_of((rows, width), F32),
            shape_of((8, width), F32),
        ),
        (by_rows(width), by_rows(width), whole((8, width))),
        [pltpu.VMEM((wide, width), BF16), pltpu.SemaphoreType.DMA],
        2 * rows * width * wide,
        "feed_out",
    )


def feed_back(info, second, slope, normed, factor, vectors, outer, inner, attn):
    rows, width = second.shape
    wide = slope.shape[1]
    part = min(1024, wide)

    def body(info_ref, ins, held, rest):
        second_ref, slope_ref, normed_ref, factor_ref, vector_ref = ins
        hidden_ref, proj_ref, mixed_ref, bias_ref, sums_ref, big, wide_m, small, sem = rest
        step = pl.program_id(0)

        @pl.when(step == 0)
        def _():
            start_load(outer, held[0], big, info_ref[0], sem.at[0])
            start_load(inner, held[1], wide_m, info_ref[0], sem.at[1])
            start_load(attn, held[2], small, info_ref[0], sem.at[2])
            sums_ref[...] = jnp.zeros_like(sums_ref)
            bias_ref[...] = jnp.zeros_like(bias_ref)
            wait_load(big, sem.at[0])

        branch = second_ref[...].astype(BF16)
        for start in range(0, wide, part):
            some = pl.ds(start, part)
            grad = dot_nt(branch, big[some, :]) * slope_ref[:, some].astype(F32)
            grad = grad.astype(BF16)
            hidden_ref[:, some] = grad
            bias_ref[0:1, some] += jnp.sum(grad.astype(F32), axis=0, keepdims=True)

        @pl.when(step == 0)
        def _():
            wait_load(wide_m, sem.at[1])
            wait_load(small, sem.at[2])

        middle = second_ref[...] + dot_nt(hidden_ref[...], wide_m[...])
        normed = normed_ref[...]
        sums_ref[0:1, :] += jnp.sum(middle * normed, axis=0, keepdims=True)
        sums_ref[1:2, :] += jnp.sum(middle, axis=0, keepdims=True)
        first = norm_back(middle * vector_ref[3:4, :], normed, factor_ref[:, 0:1])
        proj = first.astype(BF16)
        proj_ref[...] = proj
        sums_ref[2:3, :] += jnp.sum(proj.astype(F32), axis=0, keepdims=True)
        mixed_ref[...] = dot_nt(proj, small[...]).astype(BF16)

    return call(
        body,
        (rows // BLOCK,),
        info,
        (second, slope, normed, factor, vectors),
        (by_rows(width), by_rows(wide), by_rows(width), by_rows(128), whole(vectors.shape)),
        [outer, inner, attn],
        (
            shape_of((rows, wide), BF16),
            shape_of((rows, width), BF16),
            shape_of((rows, width), BF16),
            shape_of((8, wide), F32),
            shape_of((8, width), F32),
        ),
        (by_rows(wide), by_rows(width), by_rows(width), whole((8, wide)), whole((8, width))),
        [
            pltpu.VMEM((wide, width), BF16),
            pltpu.VMEM((width, wide), BF16),
            pltpu.VMEM((width, width), BF16),
            pltpu.SemaphoreType.DMA((3,)),
        ],
        4 * rows * width * wide + 2 * rows * width * width,
        "feed_back",
    )


def input_back(info, proj, steps, weights):
    rows, width = proj.shape

    def body(info_ref, ins, held, rest):
        proj_ref, step_ref = ins
        out_ref, matrix, sem = rest

        @pl.when(pl.program_id(0) == 0)
        def _():
            for i, weight in enumerate(weights):
                start_load(weight, held[i], matrix.at[i], info_ref[0], sem.at[i])
            for i in range(3):
                wait_load(matrix.at[i], sem.at[i])

        total = proj_ref[...].astype(F32)
        for i in range(3):
            total += dot_nt(step_ref[i], matrix[i])
        out_ref[...] = total.astype(BF16)

    return call(
        body,
        (rows // BLOCK,),
        info,
        (proj, steps),
        (by_rows(width), pl.BlockSpec((3, BLOCK, width), lambda i, *_: (0, i, 0))),
        weights,
        shape_of((rows, width), BF16),
        by_rows(width),
        [pltpu.VMEM((3, width, width), BF16), pltpu.SemaphoreType.DMA((3,))],
        6 * rows * width * width,
        "input_back",
    )


def weight_grad(info, left, right, places, name):
    rows, height = left.shape
    if right.ndim == 2:
        right = right[None]
    parts, _, width = right.shape
    tall = height // places
    slot = tall // 8
    part = min(1024, width)
    chunk = max(slot, 256)

    def body(info_ref, ins, held, rest):
        left_ref, right_ref = ins
        keep_ref, send_ref, held_ref = rest
        here = info_ref[0]
        for start in range(0, tall, chunk):
            total = dot_tn(left_ref[:, start : start + chunk], right_ref[0].astype(BF16))
            for k in range(chunk // slot):
                held_ref[start // slot + k] = total[k * slot : (k + 1) * slot].astype(BF16)
        core = here & 1
        for side in range(4):
            place = ((here >> 1) & 3) ^ side
            keep_ref[side, 0] = held_ref[2 * place + core]
            send_ref[side, 0] = held_ref[2 * place + 1 - core]

    out = shape_of((4, places, parts * slot, width), BF16)
    block = pl.BlockSpec((4, 1, slot, part), lambda z, w, c, *_: (0, z, w, c))
    return call(
        body,
        (places, parts, width // part),
        info,
        (left, right),
        (
            pl.BlockSpec((rows, tall), lambda z, w, c, info: (0, z ^ (info[0] >> 3))),
            pl.BlockSpec((1, rows, part), lambda z, w, c, *_: (w, 0, c)),
        ),
        [],
        (out, out),
        (block, block),
        [pltpu.VMEM((8, slot, part), BF16)],
        2 * rows * height * parts * width,
        name,
    )


def per_device(
    tokens,
    lengths,
    cotangent,
    query_weight,
    query_bias,
    key_weight,
    value_weight,
    value_bias,
    attn_weight,
    attn_bias,
    first_gain,
    first_shift,
    inner_weight,
    inner_bias,
    outer_weight,
    outer_bias,
    second_gain,
    second_shift,
):
    n = lax.axis_size("fsdp")
    here = lax.axis_index("fsdp").astype(jnp.int32)
    seqs = lengths.shape[0]
    rows, width = tokens.shape
    wide = inner_weight.shape[1]
    span = rows // seqs
    own = query_weight.shape[0]
    tall = outer_weight.shape[0]
    staged = n in (8, 16, 32) and own % 16 == 0
    info = jnp.concatenate([here[None], lengths])

    small = (
        query_bias,
        value_bias,
        attn_bias,
        first_gain,
        first_shift,
        outer_bias,
        second_gain,
        second_shift,
        inner_bias,
    )
    small = jnp.concatenate(small)[None]
    table = lax.dynamic_update_slice(jnp.zeros((n, small.shape[1]), BF16), small, (here, 0))
    table = sum_everywhere(table).astype(F32)
    vectors = table[:, : 8 * own].reshape(n, 8, own).transpose(1, 0, 2).reshape(8, width)
    wide_bias = table[:, 8 * own :].reshape(1, wide)

    if staged:
        one = jnp.concatenate([query_weight, key_weight, value_weight])
        pieces, got = gather_pieces(one, 2)
        qkv_weights = [Weight(pieces, 3 * own, i * own, own, width, width) for i in range(3)]
        pieces, got = gather_pieces(after(attn_weight, got), 4)
        attn = Weight(pieces, own, 0, own, width, width)
        pieces, got = gather_pieces(after(inner_weight, got), 4)
        inner = Weight(pieces, own, 0, own, width, wide)
        pieces, got = gather_pieces(after(outer_weight, got), 2)
        outer = Weight(pieces, tall, 0, tall, wide, width)
    else:
        full = lambda w: lax.all_gather(w, "fsdp", axis=0, tiled=True)
        view = lambda w: Weight((full(w),), 0, 0, w.shape[0], n * w.shape[0], w.shape[1])
        qkv_weights = [view(w) for w in (query_weight, key_weight, value_weight)]
        attn, inner, outer = view(attn_weight), view(inner_weight), view(outer_weight)

    biases = jnp.stack([vectors[0:1], jnp.zeros((1, width), F32), vectors[1:2]])
    qkv = project_qkv(info, tokens, biases, qkv_weights)
    mixed, logsum = attend(info, qkv, seqs)
    normed, low, factor = project_out(info, mixed, tokens, vectors, attn)
    active, slope = feed_in(info, low, wide_bias, inner)
    output, second, sums_second = feed_out(info, active, normed, cotangent, vectors, outer, span)

    def reduced(left, right, name, through):
        if staged:
            keep, send = weight_grad(info, left, right, n // 8, name)
            return scatter_pieces(keep, send, through)
        right = right if right.ndim == 3 else right[None]
        sums = [dot_tn(left, r.astype(BF16)) for r in right]
        out = [lax.psum_scatter(s, "fsdp", scatter_dimension=0, tiled=True) for s in sums]
        return jnp.concatenate(out)

    outer_wgrad = reduced(active, second.astype(BF16), "grad_outer", 2)
    grad_hidden, grad_proj, grad_mixed, sums_wide, sums_first = feed_back(
        info, second, slope, normed, factor, vectors, outer, inner, attn
    )
    inner_wgrad = reduced(low, grad_hidden, "grad_inner", 4)
    attn_wgrad = reduced(mixed, grad_proj, "grad_attn", 4)
    steps, sums_attn = attend_back(info, qkv, grad_mixed, logsum, seqs)
    qkv_wgrad = reduced(tokens, steps, "grad_qkv", 2)
    input_grad = input_back(info, grad_proj, steps, qkv_weights)

    early = jnp.concatenate([sums_second[:3], sums_first[:3], sums_wide[:1].reshape(-1, width)])
    early = sum_everywhere(early)
    late = sum_everywhere(jnp.sum(sums_attn, axis=0)[:2])
    mine = lax.dynamic_slice(early[:6], (0, here * own), (6, own))
    inner_bgrad = lax.dynamic_slice(early[6:].reshape(-1), (here * tall,), (tall,))
    last = lax.dynamic_slice(late, (0, here * own), (2, own))
    return (
        output,
        input_grad,
        qkv_wgrad[:own],
        last[0],
        qkv_wgrad[own : 2 * own],
        qkv_wgrad[2 * own :],
        last[1],
        attn_wgrad,
        mine[5],
        mine[3],
        mine[4],
        inner_wgrad,
        inner_bgrad,
        outer_wgrad,
        mine[2],
        mine[0],
        mine[1],
    )


def solution(mesh):
    rows, vector = P("fsdp", None), P("fsdp")
    return jax.shard_map(
        per_device,
        mesh=mesh,
        in_specs=(
            rows,
            vector,
            rows,
            rows,
            vector,
            rows,
            rows,
            vector,
            rows,
            vector,
            vector,
            vector,
            rows,
            vector,
            rows,
            vector,
            vector,
            vector,
        ),
        out_specs=(
            rows,
            rows,
            rows,
            vector,
            rows,
            rows,
            vector,
            rows,
            vector,
            vector,
            vector,
            rows,
            vector,
            rows,
            vector,
            vector,
            vector,
        ),
        check_vma=False,
    )
```

```python
import math

import jax
import jax.numpy as jnp
from jax import lax
from jax.experimental import pallas as pl
from jax.experimental.pallas import tpu as pltpu
from jax.sharding import PartitionSpec as P

HEADS = 16
DHEAD = 64
EPSILON = 1e-05
MASKED = -1e30
SCALE = DHEAD ** (-0.5)
F32 = jnp.float32
BF16 = jnp.bfloat16
BLOCK = 256
TALL = 256
SUB = 128
SPARE = 10 * 1024 * 1024
ROOM = 60 * 1024 * 1024
PIECES = pl.ANY
SIDES = (0, 2, 4, 6)


def dot(left, right):
    return jnp.dot(left, right, preferred_element_type=F32)


def dot_nt(left, right):
    return lax.dot_general(left, right, (((1,), (1,)), ((), ())), preferred_element_type=F32)


def dot_tn(left, right):
    return lax.dot_general(left, right, (((0,), (0,)), ((), ())), preferred_element_type=F32)


def normalize(rows):
    centred = rows - jnp.mean(rows, axis=-1, keepdims=True)
    factor = lax.rsqrt(jnp.mean(centred * centred, axis=-1, keepdims=True) + EPSILON)
    return centred * factor, factor


def norm_back(grad, normed, factor):
    mean_one = jnp.mean(grad, axis=-1, keepdims=True)
    mean_two = jnp.mean(grad * normed, axis=-1, keepdims=True)
    return factor * (grad - mean_one - normed * mean_two)


def flip(array, bits):
    n = lax.axis_size("fsdp")
    return lax.ppermute(array, "fsdp", [(i, i ^ bits) for i in range(n)])


def hold(*values):
    return lax.optimization_barrier(values)


class Weight:
    def __init__(self, pieces, slot, offset, count, rows, columns, first=0):
        self.pieces, self.slot, self.offset, self.count = pieces, slot, offset, count
        self.rows, self.columns, self.first = rows, columns, first


def gather_line(shard):
    n = lax.axis_size("fsdp")
    return [flip(shard, 8 * k) for k in range(1, n // 8)]


def gather_sides(line):
    return flip(line, 2), flip(line, 4)


def gather_across(beside, above):
    half = beside.shape[0] // 2
    return flip(above[:half], 2), flip(beside[half:], 4)


def start_load(weight, refs, target, here, sem, chunks=0):
    if len(refs) == 1:
        tall = weight.rows // max(chunks, 1)
        columns = pl.ds(weight.first, weight.columns)
        for i in range(max(chunks, 1)):
            some = pl.ds(i * tall, tall)
            pltpu.make_async_copy(
                refs[0].at[some, columns], target.at[some], sem.at[i] if chunks else sem
            ).start()
        return
    count = weight.count
    places = weight.rows // count // 8
    spots = [(side, range(places)) for side in SIDES[:3]]
    spots += [(SIDES[3], range(places // 2)), (SIDES[3], range(places // 2, places))]
    spots += [(side ^ 1, which) for side, which in spots]
    for (low, which), ref in zip(spots, refs):
        for position, k in enumerate(which):
            owner = here ^ (low ^ (8 * k))
            pltpu.make_async_copy(
                ref.at[pl.ds(position * weight.slot + weight.offset, count)],
                target.at[pl.ds(pl.multiple_of(owner * count, count), count)],
                sem.at[(owner >> 3) * chunks // places] if chunks else sem,
            ).start()


def chunk_rows(weight, chunks):
    tall = weight.rows // chunks
    return [pl.ds(i * tall, tall) for i in range(chunks)]


def wait_load(target, sem):
    pltpu.make_async_copy(target, target, sem).wait()


def sum_everywhere(array):
    n = lax.axis_size("fsdp")
    bit = 1
    while bit < n:
        array = array + flip(array, bit)
        bit *= 2
    return array


def sum_round(array, flips):
    return sum([flip(array, bits) for bits in flips], array)


def add_low(*arrays):
    total = arrays[0].astype(F32)
    for array in arrays[1:]:
        total = total + array.astype(F32)
    return total


def low_sum(*arrays):
    return add_low(*arrays).astype(BF16)


def sides_of(keep, got):
    half = max(keep.shape[1] // 2, 1)
    parts = ((3, 0), (3, half), (1, 0), (2, half), (1, half), (2, 0))
    return [low_sum(keep[s, p : p + half], got[s, p : p + half]) for s, p in parts]


def flip_first(sides):
    return flip(sides[0], 2), flip(sides[1], 4), flip(sides[2], 2), flip(sides[3], 4)


def flip_second(sides, first):
    return flip(low_sum(sides[4], first[1]), 2), flip(low_sum(sides[5], first[0]), 4)


def flip_diagonal(keep, got):
    half = max(keep.shape[1] // 2, 1)
    low = lambda p: low_sum(keep[3, p : p + half], got[3, p : p + half])
    return flip(low(0), 2), flip(low(half), 4)


def flip_whole(keep, got, moved):
    half = max(keep.shape[1] // 2, 1)
    beside = [low_sum(keep[1, :half], got[1, :half]), low_sum(keep[1, half:], got[1, half:], moved[1])]
    above = [low_sum(keep[2, :half], got[2, :half], moved[0]), low_sum(keep[2, half:], got[2, half:])]
    beside, above = flip(jnp.concatenate(beside), 2), flip(jnp.concatenate(above), 4)
    return (None, None, beside[:half], above[half:]), (beside[half:], above[:half])


def flip_line(keep, got, first, second):
    places = keep.shape[1]
    half = max(places // 2, 1)
    pieces = []
    for k in range(places):
        pair = (first[2][k], second[1][k]) if k < half else (second[0][k - half], first[3][k - half])
        pieces.append(add_low(keep[0, k], got[0, k], *pair))
    arrived = [flip(pieces[k].astype(BF16), 8 * k) for k in range(1, places)]
    return pieces[0], arrived


def operands_of(weights):
    arrays, where = [], []
    for weight in weights:
        places = []
        for piece in weight.pieces:
            for position, array in enumerate(arrays):
                if array is piece:
                    places.append(position)
                    break
            else:
                places.append(len(arrays))
                arrays.append(piece)
        where.append(places)
    return arrays, where


def call(body, grid, info, inputs, specs, weights, outs, out_specs, scratch, flops, name, exps=0, aliases={}):
    arrays, where = operands_of(weights)
    count = len(inputs)

    def kernel(info_ref, *refs):
        ins = refs[:count]
        pieces = refs[count : count + len(arrays)]
        held = [[pieces[p] for p in places] for places in where]
        body(info_ref, ins, held, refs[count + len(arrays) :])

    room = SPARE
    flat = list(zip(specs, inputs)) + list(zip(jax.tree.leaves(out_specs), jax.tree.leaves(outs)))
    for spec, array in flat:
        if spec.block_shape is not None:
            room += 2 * math.prod(spec.block_shape) * array.dtype.itemsize
    for held in scratch:
        if getattr(held, "shape", None) and held.dtype in (F32, BF16):
            room += math.prod(held.shape) * held.dtype.itemsize
    moved = sum(a.size * a.dtype.itemsize for a in list(inputs) + arrays)
    moved += sum(o.size * o.dtype.itemsize for o in jax.tree.leaves(outs))
    return pl.pallas_call(
        kernel,
        grid_spec=pltpu.PrefetchScalarGridSpec(
            num_scalar_prefetch=1,
            grid=grid,
            in_specs=list(specs) + [pl.BlockSpec(memory_space=PIECES)] * len(arrays),
            out_specs=out_specs,
            scratch_shapes=scratch,
        ),
        out_shape=outs,
        compiler_params=pltpu.CompilerParams(
            vmem_limit_bytes=max(room, ROOM), dimension_semantics=("arbitrary",) * len(grid)
        ),
        cost_estimate=pl.CostEstimate(flops=flops, bytes_accessed=moved, transcendentals=exps),
        input_output_aliases=aliases,
        name=name,
    )(info, *inputs, *arrays)


def shape_of(shape, dtype):
    return jax.ShapeDtypeStruct(shape, dtype)


def whole(shape):
    return pl.BlockSpec(shape, lambda *_: (0,) * len(shape))


def sub_blocks(rows):
    return [slice(start, start + SUB) for start in range(0, rows, SUB)]


def by_rows(columns, rows=BLOCK):
    return pl.BlockSpec((rows, columns), lambda i, *_: (i, 0))


def stacked(arrays, columns):
    rows = [array.shape[0] for array in arrays for _ in range(array.shape[1] // columns)]

    def kernel(*refs):
        out_ref, start = refs[-1], 0
        for ref in refs[:-1]:
            for first in range(0, ref.shape[1], columns):
                out_ref[start : start + ref.shape[0], :] = ref[:, first : first + columns]
                start += ref.shape[0]

    return pl.pallas_call(
        kernel,
        out_shape=shape_of((sum(rows), columns), arrays[0].dtype),
        name="stacked",
    )(*arrays)


def project_qkv(info, tokens, biases, weights):
    rows, width = tokens.shape

    def body(info_ref, ins, held, rest):
        tokens_ref, bias_ref = ins
        out_ref, matrix, sem = rest
        which = pl.program_id(0)

        @pl.when(which == 0)
        def _():
            for i, weight in enumerate(weights):
                start_load(weight, held[i], matrix.at[i], info_ref[0], sem.at[i])

        wait_load(matrix.at[which], sem.at[which])
        factor = jnp.where(which == 0, SCALE, 1.0).astype(F32)
        for start in range(0, rows, BLOCK):
            part = pl.ds(start, BLOCK)
            total = dot(tokens_ref[part, :], matrix[which]) + bias_ref[0]
            out_ref[0, part, :] = (total * factor).astype(BF16)

    return call(
        body,
        (3,),
        info,
        (tokens, biases),
        (whole(tokens.shape), pl.BlockSpec((1, 1, width), lambda i, *_: (i, 0, 0))),
        weights,
        shape_of((3, rows, width), BF16),
        pl.BlockSpec((1, rows, width), lambda i, *_: (i, 0, 0)),
        [pltpu.VMEM((3, width, width), BF16), pltpu.SemaphoreType.DMA((3,))],
        6 * rows * width * width,
        "project_qkv",
    )


def head_masks(span, length):
    lane = lax.broadcasted_iota(jnp.int32, (span, 2 * DHEAD), 1)
    place = lax.broadcasted_iota(jnp.int32, (span, 2 * DHEAD), 0)
    return lane, jnp.where(place < length, 0.0, MASKED).astype(F32)


def marked(array, lane, head, mark):
    own = lane // DHEAD == head
    spare = lane == (1 - head) * DHEAD
    return jnp.where(own, array.astype(F32), jnp.where(spare, mark, 0.0)).astype(BF16)


def attend(info, qkv, seqs, which, before):
    _, rows, width = qkv.shape
    span = rows // seqs
    pairs = width // (2 * DHEAD)

    def body(info_ref, ins, held, rest):
        query_ref, key_ref, value_ref = ins[:3]
        mixed_ref, logsum_ref = rest
        length = info_ref[1 + which]
        lane, mark = head_masks(span, length)
        query, keys = query_ref[0], key_ref[0]
        value_t = value_ref[0].T
        mixed = []
        for head in range(2):
            key_one = marked(keys, lane, head, mark)
            query_one = marked(query, lane, head, 1.0)
            scores = dot_nt(key_one, query_one)
            top = jnp.max(scores, axis=0, keepdims=True)
            expo = jnp.exp(scores - top)
            total = jnp.sum(expo, axis=0, keepdims=True)
            out = dot(value_t[head * DHEAD : (head + 1) * DHEAD], expo.astype(BF16))
            mixed.append(out / total)
            logsum_ref[0, 0, head : head + 1, :] = top + jnp.log(total)
        mixed_ref[...] = jnp.concatenate(mixed, axis=0).T.astype(BF16)

    def block(part):
        return pl.BlockSpec((1, span, 2 * DHEAD), lambda p, *_: (part, which, p))

    return call(
        body,
        (pairs,),
        info,
        (qkv, qkv, qkv) + before,
        [block(i) for i in range(3)] + [pl.BlockSpec(memory_space=pl.ANY)] * len(before),
        [],
        (shape_of((rows, width), BF16), shape_of((seqs, pairs, 8, span), F32)),
        (
            pl.BlockSpec((span, 2 * DHEAD), lambda p, *_: (which, p)),
            pl.BlockSpec((1, 1, 8, span), lambda p, *_: (which, p, 0, 0)),
        ),
        [],
        8 * span * span * width,
        "attend",
        exps=span * span * HEADS,
        aliases={4: 0, 5: 1} if before else {},
    )


def attend_back(info, qkv, grad_mixed, logsum, seqs, which, steps):
    _, rows, width = qkv.shape
    span = rows // seqs
    pairs = width // (2 * DHEAD)

    def body(info_ref, ins, held, rest):
        query_ref, key_ref, value_ref, grad_ref, logsum_ref = ins[:5]
        step_ref, sums_ref = rest
        length = info_ref[1 + which]
        lane, mark = head_masks(span, length)
        query, keys, values, grad = query_ref[0], key_ref[0], value_ref[0], grad_ref[...]
        key_t = keys.T
        query_steps, key_steps, value_steps = [], [], []
        for head in range(2):
            key_one = marked(keys, lane, head, mark)
            query_one = marked(query, lane, head, 1.0)
            value_one = marked(values, lane, head, 0.0)
            scores = dot_nt(key_one, query_one)
            probs = jnp.exp(scores - logsum_ref[0, 0, head : head + 1, :])
            grad_probs = dot_nt(value_one, grad)
            value_steps.append(dot(probs.astype(BF16), grad))
            inner = jnp.sum(grad_probs * probs, axis=0, keepdims=True)
            grad_scores = (probs * (grad_probs - inner)).astype(BF16)
            key_steps.append(dot(grad_scores, query))
            query_steps.append(
                dot(key_t[head * DHEAD : (head + 1) * DHEAD], grad_scores) * SCALE
            )
        first = lane < DHEAD
        query_step = jnp.concatenate(query_steps, axis=0).T.astype(BF16)
        key_step = jnp.where(first, key_steps[0], key_steps[1]).astype(BF16)
        value_step = jnp.where(first, value_steps[0], value_steps[1]).astype(BF16)
        step_ref[0] = query_step
        step_ref[1] = key_step
        step_ref[2] = value_step
        sums_ref[0:1, :] = jnp.sum(query_step.astype(F32), axis=0, keepdims=True)
        sums_ref[1:2, :] = jnp.sum(value_step.astype(F32), axis=0, keepdims=True)

    def block(part):
        return pl.BlockSpec((1, span, 2 * DHEAD), lambda p, *_: (part, which, p))

    return call(
        body,
        (pairs,),
        info,
        (qkv, qkv, qkv, grad_mixed, logsum) + (() if steps is None else (steps,)),
        [block(i) for i in range(3)]
        + [
            pl.BlockSpec((span, 2 * DHEAD), lambda p, *_: (which, p)),
            pl.BlockSpec((1, 1, 8, span), lambda p, *_: (which, p, 0, 0)),
        ]
        + ([] if steps is None else [pl.BlockSpec(memory_space=pl.ANY)]),
        [],
        (shape_of((3, rows, width), BF16), shape_of((8, width), F32)),
        (
            pl.BlockSpec((3, span, 2 * DHEAD), lambda p, *_: (0, which, p)),
            pl.BlockSpec((8, 2 * DHEAD), lambda p, *_: (0, p)),
        ),
        [],
        10 * span * span * width * 2,
        "attend_back",
        exps=span * span * HEADS,
        aliases={} if steps is None else {6: 0},
    )


def project_out(info, mixed, tokens, vectors, weight):
    rows, width = tokens.shape

    def body(info_ref, ins, held, rest):
        mixed_ref, tokens_ref, vector_ref = ins
        normed_ref, low_ref, factor_ref, matrix, sem = rest

        @pl.when(pl.program_id(0) == 0)
        def _():
            start_load(weight, held[0], matrix, info_ref[0], sem)
            wait_load(matrix, sem)

        for part in sub_blocks(TALL):
            branch = dot(mixed_ref[part, :], matrix[...]) + vector_ref[2:3, :]
            normed, factor = normalize(tokens_ref[part, :].astype(F32) + branch)
            normed_ref[part, :] = normed.astype(BF16)
            low_ref[part, :] = (normed * vector_ref[3:4, :] + vector_ref[4:5, :]).astype(BF16)
            factor_ref[part, :] = jnp.broadcast_to(factor, (SUB, 128))

    return call(
        body,
        (rows // TALL,),
        info,
        (mixed, tokens, vectors),
        (by_rows(width, TALL), by_rows(width, TALL), whole(vectors.shape)),
        [weight],
        (shape_of((rows, width), BF16), shape_of((rows, width), BF16), shape_of((rows, 128), F32)),
        (by_rows(width, TALL), by_rows(width, TALL), by_rows(128, TALL)),
        [pltpu.VMEM((width, width), BF16), pltpu.SemaphoreType.DMA],
        2 * rows * width * width,
        "project_out",
    )


def gelu_both(hidden):
    share = 0.5 * lax.erf(hidden * 0.7071067811865476) + 0.5
    bell = jnp.exp(-0.5 * (hidden * hidden))
    return hidden * share, share + hidden * (bell * 0.3989422804014327)


def feed_in(info, low, bias, weights, begin, end, before):
    rows, width = low.shape
    part = weights[0].columns
    wide = len(weights) * part
    steps = end - begin

    def body(info_ref, ins, held, rest):
        low_ref, bias_ref = ins[:2]
        active_ref, slope_ref, matrix, sem = rest
        step = pl.program_id(0)

        @pl.when(step == 0)
        def _():
            for i in range(steps):
                start_load(weights[begin + i], held[i], matrix.at[i], info_ref[0], sem.at[i])

        wait_load(matrix.at[step], sem.at[step])
        for start in range(0, rows, BLOCK):
            some = pl.ds(start, BLOCK)
            hidden = dot(low_ref[some, :], matrix[step]) + bias_ref[...]
            active, slope = gelu_both(hidden)
            active_ref[some, :] = active.astype(BF16)
            slope_ref[some, :] = slope.astype(BF16)

    columns = pl.BlockSpec((rows, part), lambda i, *_: (0, begin + i))
    return call(
        body,
        (steps,),
        info,
        (low, bias) + before,
        (whole(low.shape), pl.BlockSpec((1, part), lambda i, *_: (0, begin + i)))
        + (pl.BlockSpec(memory_space=pl.ANY),) * len(before),
        weights[begin:end],
        (shape_of((rows, wide), BF16), shape_of((rows, wide), BF16)),
        (columns, columns),
        [pltpu.VMEM((steps, width, part), BF16), pltpu.SemaphoreType.DMA((steps,))],
        2 * rows * width * part * steps,
        "feed_in",
        exps=rows * part * steps,
        aliases={3: 0, 4: 1} if before else {},
    )


def feed_out(info, active, normed, cotangent, vectors, weight, span):
    rows, wide = active.shape
    width = weight.columns

    def body(info_ref, ins, held, rest):
        active_ref, normed_ref, cotangent_ref, vector_ref = ins
        out_ref, branch_ref, sums_ref, matrix, sem = rest
        step = pl.program_id(0)

        @pl.when(step == 0)
        def _():
            start_load(weight, held[0], matrix, info_ref[0], sem, chunks=2)
            sums_ref[...] = jnp.zeros_like(sums_ref)

        total = 0.0
        for i, some in enumerate(chunk_rows(weight, 2)):

            @pl.when(step == 0)
            def _():
                wait_load(matrix.at[some], sem.at[i])

            total += dot(active_ref[:, some], matrix[some, :])
        sequence = (step * TALL) // span
        length = info_ref[1 + sequence]
        for part in sub_blocks(TALL):
            middle = normed_ref[part, :].astype(F32) * vector_ref[3:4, :] + vector_ref[4:5, :]
            branch = total[part, :] + vector_ref[5:6, :]
            second, factor = normalize(middle + branch)
            gain = vector_ref[6:7, :]
            out_ref[part, :] = (second * gain + vector_ref[7:8, :]).astype(BF16)
            places = step * TALL + part.start + lax.broadcasted_iota(jnp.int32, (SUB, 1), 0)
            valid = places - sequence * span < length
            grad = jnp.where(valid, cotangent_ref[part, :].astype(F32), 0.0)
            sums_ref[0:1, :] += jnp.sum(grad * second, axis=0, keepdims=True)
            sums_ref[1:2, :] += jnp.sum(grad, axis=0, keepdims=True)
            back = norm_back(grad * gain, second, factor)
            branch = back.astype(BF16)
            branch_ref[part, :] = branch
            sums_ref[2:3, :] += jnp.sum(branch.astype(F32), axis=0, keepdims=True)

    return call(
        body,
        (rows // TALL,),
        info,
        (active, normed, cotangent, vectors),
        (by_rows(wide, TALL), by_rows(width, TALL), by_rows(width, TALL), whole(vectors.shape)),
        [weight],
        (
            shape_of((rows, width), BF16),
            shape_of((rows, width), BF16),
            shape_of((8, width), F32),
        ),
        (by_rows(width, TALL), by_rows(width, TALL), whole((8, width))),
        [pltpu.VMEM((wide, width), BF16), pltpu.SemaphoreType.DMA((2,))],
        2 * rows * width * wide,
        "feed_out",
    )


def hidden_back(info, branch, slope, outer):
    rows, width = branch.shape
    wide = slope.shape[1]
    steps = 2
    part = wide // steps

    def body(info_ref, ins, held, rest):
        branch_ref, slope_ref = ins
        hidden_ref, bias_ref, big, sem = rest
        step = pl.program_id(0)

        @pl.when(step == 0)
        def _():
            start_load(outer, held[0], big, info_ref[0], sem, chunks=steps)

        some = pl.ds(pl.multiple_of(step * part, part), part)
        wait_load(big.at[some], sem.at[step])
        total = jnp.zeros((8, part), F32)
        for start in range(0, rows, BLOCK):
            here = slice(start, start + BLOCK)
            grad = dot_nt(branch_ref[here, :], big[some, :]) * slope_ref[here, :].astype(F32)
            grad = grad.astype(BF16)
            hidden_ref[here, :] = grad
            total += jnp.sum(grad.astype(F32).reshape(BLOCK // 8, 8, part), axis=0)
        bias_ref[...] = jnp.broadcast_to(jnp.sum(total, axis=0, keepdims=True), bias_ref.shape)

    columns = pl.BlockSpec((rows, part), lambda i, *_: (0, i))
    return call(
        body,
        (steps,),
        info,
        (branch, slope),
        (whole(branch.shape), columns),
        [outer],
        (shape_of((rows, wide), BF16), shape_of((8, wide), F32)),
        (columns, pl.BlockSpec((8, part), lambda i, *_: (0, i))),
        [pltpu.VMEM((wide, width), BF16), pltpu.SemaphoreType.DMA((steps,))],
        2 * rows * width * wide,
        "hidden_back",
    )


def middle_back(info, branch, hidden, normed, factor, vectors, inner, attn):
    rows, width = branch.shape
    wide = hidden.shape[1]
    chunks, part = len(inner), inner[0].columns

    def body(info_ref, ins, held, rest):
        branch_ref, hidden_ref, normed_ref, factor_ref, vector_ref = ins
        proj_ref, mixed_ref, sums_ref, big, small, sem = rest
        step = pl.program_id(0)

        @pl.when(step == 0)
        def _():
            for i in range(chunks):
                start_load(inner[i], held[i], big.at[i], info_ref[0], sem.at[i])
            start_load(attn, held[chunks], small, info_ref[0], sem.at[chunks])
            sums_ref[...] = jnp.zeros_like(sums_ref)

        middle = branch_ref[...].astype(F32)
        for i in range(chunks):

            @pl.when(step == 0)
            def _():
                wait_load(big.at[i], sem.at[i])

            middle += dot_nt(hidden_ref[:, i * part : (i + 1) * part], big[i])

        @pl.when(step == 0)
        def _():
            wait_load(small, sem.at[chunks])

        normed = normed_ref[...].astype(F32)
        sums_ref[0:1, :] += jnp.sum(middle * normed, axis=0, keepdims=True)
        sums_ref[1:2, :] += jnp.sum(middle, axis=0, keepdims=True)
        first = norm_back(middle * vector_ref[3:4, :], normed, factor_ref[:, 0:1])
        proj = first.astype(BF16)
        proj_ref[...] = proj
        sums_ref[2:3, :] += jnp.sum(proj.astype(F32), axis=0, keepdims=True)
        mixed_ref[...] = dot_nt(proj, small[...]).astype(BF16)

    return call(
        body,
        (rows // BLOCK,),
        info,
        (branch, hidden, normed, factor, vectors),
        (by_rows(width), by_rows(wide), by_rows(width), by_rows(128), whole(vectors.shape)),
        inner + [attn],
        (shape_of((rows, width), BF16), shape_of((rows, width), BF16), shape_of((8, width), F32)),
        (by_rows(width), by_rows(width), whole((8, width))),
        [
            pltpu.VMEM((chunks, width, part), BF16),
            pltpu.VMEM((width, width), BF16),
            pltpu.SemaphoreType.DMA((chunks + 1,)),
        ],
        2 * rows * width * wide + 2 * rows * width * width,
        "middle_back",
    )


def input_back(info, proj, steps, weights):
    rows, width = proj.shape

    def body(info_ref, ins, held, rest):
        proj_ref, step_ref = ins
        out_ref, matrix, sem = rest

        @pl.when(pl.program_id(0) == 0)
        def _():
            for i, weight in enumerate(weights):
                start_load(weight, held[i], matrix.at[i], info_ref[0], sem.at[i])

        total = proj_ref[...].astype(F32)
        for i in range(3):

            @pl.when(pl.program_id(0) == 0)
            def _():
                wait_load(matrix.at[i], sem.at[i])

            total += dot_nt(step_ref[i], matrix[i])
        out_ref[...] = total.astype(BF16)

    return call(
        body,
        (rows // BLOCK,),
        info,
        (proj, steps),
        (by_rows(width), pl.BlockSpec((3, BLOCK, width), lambda i, *_: (0, i, 0))),
        weights,
        shape_of((rows, width), BF16),
        by_rows(width),
        [pltpu.VMEM((3, width, width), BF16), pltpu.SemaphoreType.DMA((3,))],
        6 * rows * width * width,
        "input_back",
    )


def weight_grad(info, lefts, rights, places, name):
    rows, height = lefts[0].shape
    slot = height // (8 * places)
    block = 8 * slot
    part = min(1024, rights[0].shape[-1])
    counts = [r.shape[0] if r.ndim == 3 else r.shape[1] // part for r in rights]
    firsts = [sum(counts[:i]) for i in range(len(counts))]
    parts = sum(counts)
    half = height // 2

    def body(info_ref, ins, held, rest):
        left_refs, right_refs = ins[: len(lefts)], ins[len(lefts) :]
        keep_ref, send_ref, sorted_ref = rest
        here = info_ref[0]
        step = pl.program_id(0)
        for left_ref, right_ref, first, count in zip(left_refs, right_refs, firsts, counts):

            @pl.when(step == first)
            def _():
                for z in range(places):
                    turned = left_ref[:, z * block : (z + 1) * block].T
                    for k in range(8):
                        relative = (z * 8 + k) ^ here
                        spot = (relative & 1) * 4 + ((relative >> 1) & 3)
                        spot = spot * places + (relative >> 3)
                        sorted_ref[pl.ds(pl.multiple_of(spot * slot, slot), slot), :] = turned[
                            k * slot : (k + 1) * slot
                        ]

            @pl.when((step >= first) & (step < first + count))
            def _():
                right = right_ref[0] if len(right_ref.shape) == 3 else right_ref[...]
                for out_ref, start in ((keep_ref, 0), (send_ref, half)):
                    for side in range(4):
                        size = half // 4
                        total = dot(sorted_ref[start + side * size : start + (side + 1) * size, :], right)
                        out_ref[side] = total.astype(BF16).reshape(places, slot, part)

    def right_spec(right, first, count):
        place = lambda w: jnp.clip(w - first, 0, count - 1)
        if right.ndim == 3:
            return pl.BlockSpec((1, rows, part), lambda w, *_: (place(w), 0, 0))
        return pl.BlockSpec((rows, part), lambda w, *_: (0, place(w)))

    out = shape_of((4, places, parts * slot, part), BF16)
    out_block = pl.BlockSpec((4, places, slot, part), lambda w, *_: (0, 0, w, 0))
    return call(
        body,
        (parts,),
        info,
        tuple(lefts) + tuple(rights),
        [whole(left.shape) for left in lefts]
        + [right_spec(r, f, c) for r, f, c in zip(rights, firsts, counts)],
        [],
        (out, out),
        (out_block, out_block),
        [pltpu.VMEM((height, rows), BF16)],
        2 * rows * height * parts * part,
        name,
    )


def weight_grad_tall(info, left, right, places, name):
    rows, height = left.shape
    width = right.shape[1]
    slot = height // (8 * places)

    def body(info_ref, ins, held, rest):
        left_ref, right_ref = ins
        keep_ref, send_ref = rest
        here = info_ref[0]
        for side in range(4):
            for out_ref, other in ((keep_ref, 0), (send_ref, 1)):
                which = (here & 7) ^ (2 * side + other)
                some = pl.ds(pl.multiple_of(which * slot, slot), slot)
                out_ref[side, 0] = dot_tn(left_ref[:, some], right_ref[...]).astype(BF16)

    out = shape_of((4, places, slot, width), BF16)
    block = pl.BlockSpec((4, 1, slot, width), lambda z, *_: (0, z, 0, 0))
    return call(
        body,
        (places,),
        info,
        (left, right),
        (
            pl.BlockSpec((rows, 8 * slot), lambda z, info: (0, z ^ (info[0] >> 3))),
            whole(right.shape),
        ),
        [],
        (out, out),
        (block, block),
        [],
        2 * rows * height * width,
        name,
    )


def sums_of(second, first, attn, wide):
    attn = sum(attn)[:2]
    return jnp.concatenate([second[:3], first[:3], attn, wide[:1].reshape(-1, second.shape[1])])


def per_device(
    tokens,
    lengths,
    cotangent,
    query_weight,
    query_bias,
    key_weight,
    value_weight,
    value_bias,
    attn_weight,
    attn_bias,
    first_gain,
    first_shift,
    inner_weight,
    inner_bias,
    outer_weight,
    outer_bias,
    second_gain,
    second_shift,
):
    n = lax.axis_size("fsdp")
    here = lax.axis_index("fsdp").astype(jnp.int32)
    seqs = lengths.shape[0]
    rows, width = tokens.shape
    wide = inner_weight.shape[1]
    span = rows // seqs
    own = query_weight.shape[0]
    tall = outer_weight.shape[0]
    staged = n in (16, 32) and own % 16 == 0
    info = jnp.concatenate([here[None], lengths])

    full = lambda w: lax.all_gather(w, "fsdp", axis=0, tiled=True)
    whole_weight = lambda w: Weight((w,), 0, 0, w.shape[0] // n, w.shape[0], w.shape[1])

    small = jnp.stack(
        (
            query_bias,
            value_bias,
            attn_bias,
            first_gain,
            first_shift,
            outer_bias,
            second_gain,
            second_shift,
        )
    )
    table = jnp.zeros((8 + wide // width, width), BF16)
    table = lax.dynamic_update_slice(table, small, (0, here * own))
    spot = here * tall
    table = lax.dynamic_update_slice(table, inner_bias[None], (8 + spot // width, spot % width))

    if staged:
        places = n // 8
        one = stacked([query_weight, key_weight, value_weight], width)
        two = stacked([inner_weight, attn_weight], width)
        others = gather_line(one)
        for bits in (1, 2, 4):
            table = sum_round(table, (bits,))
        table, two, *others = hold(table, two, *others)
        line = jnp.concatenate([one, *others])
        beside, above = gather_sides(line)
        cut = 3 * own
        others_top = gather_line(two[:cut])
        line, beside, above, two, *others_top = hold(line, beside, above, two, *others_top)
        others_low = gather_line(two[cut:])
        near = (line, beside, above) + gather_across(beside, above)
        table, two, *near = hold(table, two, *near, *others_low)
        near, others_low = near[:5], near[5:]
        table = sum_round(table, [8 * k for k in range(1, places)])
        pieces = near + [flip(piece, 1) for piece in near]
        line_two = jnp.concatenate([two] + [p for pair in zip(others_top, others_low) for p in pair])
        table, line_two, three, *pieces = hold(table, line_two, outer_weight, *pieces)
        qkv_weights = [Weight(pieces, 3 * own, i * own, own, width, width) for i in range(3)]
    else:
        table = sum_everywhere(table)
        qkv_weights = [whole_weight(full(w)) for w in (query_weight, key_weight, value_weight)]
        outer = whole_weight(full(outer_weight))
    table = table.astype(F32)
    vectors, wide_bias = table[:8], table[8:].reshape(1, wide)
    biases = jnp.stack([vectors[0:1], jnp.zeros((1, width), F32), vectors[1:2]])

    blocks = wide // width
    if staged:
        beside, above = gather_sides(line_two)
        others_three = gather_line(three)
        qkv = project_qkv(info, tokens, biases, qkv_weights)
        result = attend(info, qkv, seqs, 0, ())
        beside, above, *result = hold(beside, above, *others_three, *result)
        others_three, result = result[: places - 1], result[places - 1 :]
        near = (line_two, beside, above) + gather_across(beside, above)
        far = tuple(flip(piece, 1) for piece in near[:3])
        line_three = jnp.concatenate([three, *others_three])
        for which in range(1, seqs):
            result = attend(info, qkv, seqs, which, tuple(result))
        mixed, logsum, line_three, *pieces = hold(*result, line_three, *near, *far)
        beside, above = gather_sides(line_three)
        pieces = pieces + [flip(piece, 1) for piece in pieces[3:5]]
        inner = [Weight(pieces, 5 * own, i * own, own, width, width) for i in range(blocks)]
        attn = Weight(pieces, 5 * own, blocks * own, own, width, width)
        normed, low, factor = project_out(info, mixed, tokens, vectors, attn)
        active, slope = feed_in(info, low, wide_bias, inner, 0, blocks // 2, ())
        line_three, beside, above, active, slope = hold(line_three, beside, above, active, slope)
        near = (line_three, beside, above) + gather_across(beside, above)
        far = tuple(flip(piece, 1) for piece in near[:3])
        active, slope = feed_in(info, low, wide_bias, inner, blocks // 2, blocks, (active, slope))
        active, *pieces = hold(active, *near, *far)
        pieces = pieces + [flip(piece, 1) for piece in pieces[3:5]]
        outer = Weight(pieces, tall, 0, tall, wide, width)
    else:
        attn, inner = whole_weight(full(attn_weight)), full(inner_weight)
        inner = [Weight((inner,), 0, 0, own, width, width, i * width) for i in range(blocks)]
        qkv = project_qkv(info, tokens, biases, qkv_weights)
        result = ()
        for which in range(seqs):
            result = attend(info, qkv, seqs, which, tuple(result))
        mixed, logsum = result
        normed, low, factor = project_out(info, mixed, tokens, vectors, attn)
        active, slope = feed_in(info, low, wide_bias, inner, 0, blocks, ())
    output, branch, sums_second = feed_out(
        info, active, normed, cotangent, vectors, outer, span
    )

    def back_of(hidden):
        return middle_back(info, branch, hidden, normed, factor, vectors, inner, attn)

    def attend_all(grad_mixed):
        steps, sums = None, []
        for which in range(seqs):
            steps, some = attend_back(info, qkv, grad_mixed, logsum, seqs, which, steps)
            sums.append(some)
        return steps, sums

    if staged:
        keep_o, send_o = weight_grad_tall(info, active, branch, places, "grad_outer")
        keep_o, send_o, branch = hold(keep_o, send_o, branch)
        got_o = flip(send_o, 1)
        grad_hidden, sums_wide = hidden_back(info, branch, slope, outer)
        got_o, grad_hidden, sums_wide = hold(got_o, grad_hidden, sums_wide)
        sides_o = sides_of(keep_o, got_o)
        grad_hidden, *sides_o = hold(grad_hidden, *sides_o)
        first_o = flip_first(sides_o)
        grad_proj, grad_mixed, sums_first = back_of(grad_hidden)
        first_o, grad_proj, grad_mixed, sums_first = hold(
            first_o, grad_proj, grad_mixed, sums_first
        )
        second_o = flip_second(sides_o, first_o)
        keep, send = weight_grad(
            info, (low, mixed), (grad_hidden, grad_proj), places, "grad_inner_attn"
        )
        second_o, keep, send, grad_mixed = hold(second_o, keep, send, grad_mixed)
        got = flip(send, 1)
        kept_o, arrived_o = flip_line(keep_o, got_o, first_o, second_o)
        steps, some = attend_back(info, qkv, grad_mixed, logsum, seqs, 0, None)
        sums_attn = [some]
        got, kept_o, arrived_o, steps = hold(got, kept_o, arrived_o, steps)
        sides = sides_of(keep, got)
        outer_wgrad = add_low(kept_o, *arrived_o)
        steps, outer_wgrad, *sides = hold(steps, outer_wgrad, *sides)
        first = flip_first(sides)
        for which in range(1, seqs):
            steps, some = attend_back(info, qkv, grad_mixed, logsum, seqs, which, steps)
            sums_attn.append(some)
        keep_two, send_two = weight_grad(info, (tokens,), (steps,), places, "grad_qkv")
        first, steps, keep_two, send_two, *sums_attn = hold(
            first, steps, keep_two, send_two, *sums_attn
        )
        got_two = flip(send_two, 1)
        sums = sums_of(sums_second, sums_first, sums_attn, sums_wide)
        sums = sum_round(sums, (1,))
        second = flip_second(sides, first)
        input_grad = input_back(info, grad_proj, steps, qkv_weights)
        got_two, sums, second, input_grad = hold(got_two, sums, second, input_grad)
        moved_two = flip_diagonal(keep_two, got_two)
        sums = sum_round(sums, [8 * k for k in range(1, places)])
        sums, keep, *moved_two = hold(sums, keep, *moved_two)
        first_two, second_two = flip_whole(keep_two, got_two, moved_two)
        kept, arrived = flip_line(keep, got, first, second)
        sums, first_two, second_two = hold(sums, first_two, second_two)
        sums = sum_round(sum_round(sums, (2,)), (4,))
        kept_two, arrived_two = flip_line(keep_two, got_two, first_two, second_two)
        both = add_low(kept, *arrived)
        qkv_wgrad = add_low(kept_two, *arrived_two)
        attn_wgrad = both[wide // width * own :]
        inner_wgrad = both[: wide // width * own].reshape(wide // width, own, width)
        inner_wgrad = inner_wgrad.transpose(1, 0, 2).reshape(own, wide)
    else:
        scatter = lambda g: lax.psum_scatter(g, "fsdp", scatter_dimension=0, tiled=True)
        outer_wgrad = scatter(dot_tn(active, branch))
        grad_hidden, sums_wide = hidden_back(info, branch, slope, outer)
        grad_proj, grad_mixed, sums_first = back_of(grad_hidden)
        steps, sums_attn = attend_all(grad_mixed)
        input_grad = input_back(info, grad_proj, steps, qkv_weights)
        inner_wgrad = scatter(dot_tn(low, grad_hidden))
        attn_wgrad = scatter(dot_tn(mixed, grad_proj))
        qkv_wgrad = jnp.concatenate([scatter(dot_tn(tokens, steps[i])) for i in range(3)])
        sums = sum_everywhere(sums_of(sums_second, sums_first, sums_attn, sums_wide))

    mine = lax.dynamic_slice(sums, (0, here * own), (8, own))
    inner_bgrad = lax.dynamic_slice(sums, (8 + spot // width, spot % width), (1, tall))[0]
    return (
        output,
        input_grad,
        qkv_wgrad[:own],
        mine[6],
        qkv_wgrad[own : 2 * own],
        qkv_wgrad[2 * own :],
        mine[7],
        attn_wgrad,
        mine[5],
        mine[3],
        mine[4],
        inner_wgrad,
        inner_bgrad,
        outer_wgrad,
        mine[2],
        mine[0],
        mine[1],
    )


def solution(mesh):
    rows, vector = P("fsdp", None), P("fsdp")
    return jax.shard_map(
        per_device,
        mesh=mesh,
        in_specs=(
            rows,
            vector,
            rows,
            rows,
            vector,
            rows,
            rows,
            vector,
            rows,
            vector,
            vector,
            vector,
            rows,
            vector,
            rows,
            vector,
            vector,
            vector,
        ),
        out_specs=(
            rows,
            rows,
            rows,
            vector,
            rows,
            rows,
            vector,
            rows,
            vector,
            vector,
            vector,
            rows,
            vector,
            rows,
            vector,
            vector,
            vector,
        ),
        check_vma=False,
    )
```

```python
import math

import jax
import jax.numpy as jnp
from jax import lax
from jax.experimental import pallas as pl
from jax.experimental.pallas import tpu as pltpu
from jax.sharding import PartitionSpec as P

HEADS = 16
DHEAD = 64
EPSILON = 1e-05
MASKED = -1e30
SCALE = DHEAD ** (-0.5)
F32 = jnp.float32
BF16 = jnp.bfloat16
BLOCK = 256
TALL = 256
SUB = 128
SPARE = 10 * 1024 * 1024
ROOM = 60 * 1024 * 1024
PIECES = pltpu.HBM
TIGHT = ("attend_back", "grad_qkv")
SIDES = (0, 2, 4, 6)


def dot(left, right):
    return jnp.dot(left, right, preferred_element_type=F32)


def dot_nt(left, right):
    return lax.dot_general(left, right, (((1,), (1,)), ((), ())), preferred_element_type=F32)


def dot_tn(left, right):
    return lax.dot_general(left, right, (((0,), (0,)), ((), ())), preferred_element_type=F32)


def normalize(rows):
    centred = rows - jnp.mean(rows, axis=-1, keepdims=True)
    factor = lax.rsqrt(jnp.mean(centred * centred, axis=-1, keepdims=True) + EPSILON)
    return centred * factor, factor


def norm_back(grad, normed, factor):
    mean_one = jnp.mean(grad, axis=-1, keepdims=True)
    mean_two = jnp.mean(grad * normed, axis=-1, keepdims=True)
    return factor * (grad - mean_one - normed * mean_two)


def flip(array, bits):
    n = lax.axis_size("fsdp")
    return lax.ppermute(array, "fsdp", [(i, i ^ bits) for i in range(n)])


def hold(*values):
    return lax.optimization_barrier(values)


class Weight:
    def __init__(self, pieces, slot, offset, count, rows, columns, first=0):
        self.pieces, self.slot, self.offset, self.count = pieces, slot, offset, count
        self.rows, self.columns, self.first = rows, columns, first


def gather_line(shard):
    n = lax.axis_size("fsdp")
    return [flip(shard, 8 * k) for k in range(1, n // 8)]


def gather_sides(line):
    return flip(line, 2), flip(line, 4)


def gather_across(beside, above):
    half = beside.shape[0] // 2
    return flip(above[:half], 2), flip(beside[half:], 4)


def start_load(weight, refs, target, here, sem, chunks=0):
    if len(refs) == 1:
        tall = weight.rows // max(chunks, 1)
        columns = pl.ds(weight.first, weight.columns)
        for i in range(max(chunks, 1)):
            some = pl.ds(i * tall, tall)
            pltpu.make_async_copy(
                refs[0].at[some, columns], target.at[some], sem.at[i] if chunks else sem
            ).start()
        return
    count = weight.count
    places = weight.rows // count // 8
    spots = [(side, range(places)) for side in SIDES[:3]]
    spots += [(SIDES[3], range(places // 2)), (SIDES[3], range(places // 2, places))]
    spots += [(side ^ 1, which) for side, which in spots]
    for (low, which), ref in zip(spots, refs):
        for position, k in enumerate(which):
            owner = here ^ (low ^ (8 * k))
            pltpu.make_async_copy(
                ref.at[pl.ds(position * weight.slot + weight.offset, count)],
                target.at[pl.ds(pl.multiple_of(owner * count, count), count)],
                sem.at[(owner >> 3) * chunks // places] if chunks else sem,
            ).start()


def chunks_of(weight):
    return 4 if len(weight.pieces) == 1 else weight.rows // weight.count // 8


def wait_load(target, sem):
    pltpu.make_async_copy(target, target, sem).wait()


def sum_everywhere(array):
    n = lax.axis_size("fsdp")
    bit = 1
    while bit < n:
        array = array + flip(array, bit)
        bit *= 2
    return array


def sum_round(array, flips):
    return sum([flip(array, bits) for bits in flips], array)


def add_low(*arrays):
    total = arrays[0].astype(F32)
    for array in arrays[1:]:
        total = total + array.astype(F32)
    return total


def low_sum(*arrays):
    return add_low(*arrays).astype(BF16)


def sides_of(keep, got):
    half = max(keep.shape[1] // 2, 1)
    parts = ((3, 0), (3, half), (1, 0), (2, half), (1, half), (2, 0))
    return [low_sum(keep[s, p : p + half], got[s, p : p + half]) for s, p in parts]


def flip_first(sides):
    return flip(sides[0], 2), flip(sides[1], 4), flip(sides[2], 2), flip(sides[3], 4)


def flip_second(sides, first):
    return flip(low_sum(sides[4], first[1]), 2), flip(low_sum(sides[5], first[0]), 4)


def flip_diagonal(keep, got):
    half = max(keep.shape[1] // 2, 1)
    low = lambda p: low_sum(keep[3, p : p + half], got[3, p : p + half])
    return flip(low(0), 2), flip(low(half), 4)


def flip_whole(keep, got, moved):
    half = max(keep.shape[1] // 2, 1)
    beside = [low_sum(keep[1, :half], got[1, :half]), low_sum(keep[1, half:], got[1, half:], moved[1])]
    above = [low_sum(keep[2, :half], got[2, :half], moved[0]), low_sum(keep[2, half:], got[2, half:])]
    beside, above = flip(jnp.concatenate(beside), 2), flip(jnp.concatenate(above), 4)
    return (None, None, beside[:half], above[half:]), (beside[half:], above[:half])


def flip_line(keep, got, first, second):
    places = keep.shape[1]
    half = max(places // 2, 1)
    pieces = []
    for k in range(places):
        pair = (first[2][k], second[1][k]) if k < half else (second[0][k - half], first[3][k - half])
        pieces.append(add_low(keep[0, k], got[0, k], *pair))
    arrived = [flip(pieces[k].astype(BF16), 8 * k) for k in range(1, places)]
    return pieces[0], arrived


def operands_of(weights):
    arrays, where = [], []
    for weight in weights:
        places = []
        for piece in weight.pieces:
            for position, array in enumerate(arrays):
                if array is piece:
                    places.append(position)
                    break
            else:
                places.append(len(arrays))
                arrays.append(piece)
        where.append(places)
    return arrays, where


def call(body, grid, info, inputs, specs, weights, outs, out_specs, scratch, flops, name, exps=0, aliases={}):
    arrays, where = operands_of(weights)
    count = len(inputs)

    def kernel(info_ref, *refs):
        ins = refs[:count]
        pieces = refs[count : count + len(arrays)]
        held = [[pieces[p] for p in places] for places in where]
        body(info_ref, ins, held, refs[count + len(arrays) :])

    room = SPARE
    flat = list(zip(specs, inputs)) + list(zip(jax.tree.leaves(out_specs), jax.tree.leaves(outs)))
    for spec, array in flat:
        if spec.block_shape is not None:
            room += 2 * math.prod(spec.block_shape) * array.dtype.itemsize
    for held in scratch:
        if getattr(held, "shape", None) and held.dtype in (F32, BF16):
            room += math.prod(held.shape) * held.dtype.itemsize
    moved = sum(a.size * a.dtype.itemsize for a in list(inputs) + arrays)
    moved += sum(o.size * o.dtype.itemsize for o in jax.tree.leaves(outs))
    return pl.pallas_call(
        kernel,
        grid_spec=pltpu.PrefetchScalarGridSpec(
            num_scalar_prefetch=1,
            grid=grid,
            in_specs=list(specs) + [pl.BlockSpec(memory_space=PIECES)] * len(arrays),
            out_specs=out_specs,
            scratch_shapes=scratch,
        ),
        out_shape=outs,
        compiler_params=pltpu.CompilerParams(
            vmem_limit_bytes=room if name in TIGHT else ROOM, dimension_semantics=("arbitrary",) * len(grid)
        ),
        cost_estimate=pl.CostEstimate(flops=flops, bytes_accessed=moved, transcendentals=exps),
        input_output_aliases=aliases,
        name=name,
    )(info, *inputs, *arrays)


def shape_of(shape, dtype):
    return jax.ShapeDtypeStruct(shape, dtype)


def whole(shape):
    return pl.BlockSpec(shape, lambda *_: (0,) * len(shape))


def sub_blocks(rows):
    return [slice(start, start + SUB) for start in range(0, rows, SUB)]


def by_rows(columns, rows=BLOCK):
    return pl.BlockSpec((rows, columns), lambda i, *_: (i, 0))


def stacked(arrays, columns):
    rows = [array.shape[0] for array in arrays for _ in range(array.shape[1] // columns)]

    def kernel(*refs):
        out_ref, start = refs[-1], 0
        for ref in refs[:-1]:
            for first in range(0, ref.shape[1], columns):
                out_ref[start : start + ref.shape[0], :] = ref[:, first : first + columns]
                start += ref.shape[0]

    return pl.pallas_call(
        kernel,
        out_shape=shape_of((sum(rows), columns), arrays[0].dtype),
        name="stacked",
    )(*arrays)


def project_qkv(info, tokens, biases, weights):
    rows, width = tokens.shape

    def body(info_ref, ins, held, rest):
        tokens_ref, bias_ref = ins
        out_ref, matrix, sem = rest
        which = pl.program_id(0)

        @pl.when(which == 0)
        def _():
            start_load(weights[0], held[0], matrix.at[0], info_ref[0], sem.at[0])

        wait_load(matrix.at[which], sem.at[which])
        for i in range(1, 3):

            @pl.when(which == i - 1)
            def _():
                start_load(weights[i], held[i], matrix.at[i], info_ref[0], sem.at[i])

        factor = jnp.where(which == 0, SCALE, 1.0).astype(F32)
        for start in range(0, rows, BLOCK):
            part = pl.ds(start, BLOCK)
            total = dot(tokens_ref[part, :], matrix[which]) + bias_ref[0]
            out_ref[0, part, :] = (total * factor).astype(BF16)

    return call(
        body,
        (3,),
        info,
        (tokens, biases),
        (whole(tokens.shape), pl.BlockSpec((1, 1, width), lambda i, *_: (i, 0, 0))),
        weights,
        shape_of((3, rows, width), BF16),
        pl.BlockSpec((1, rows, width), lambda i, *_: (i, 0, 0)),
        [pltpu.VMEM((3, width, width), BF16), pltpu.SemaphoreType.DMA((3,))],
        6 * rows * width * width,
        "project_qkv",
    )


def head_rows():
    lane = lax.broadcasted_iota(jnp.int32, (1, 2 * DHEAD), 1)
    own = [(lane // DHEAD == head).astype(F32).astype(BF16) for head in range(2)]
    spare = [(lane == (1 - head) * DHEAD).astype(F32).astype(BF16) for head in range(2)]
    return own, spare


def fill_marks(mark_ref, length):
    shape = mark_ref.shape[1:]
    lane = lax.broadcasted_iota(jnp.int32, shape, 1)
    masked = lax.broadcasted_iota(jnp.int32, shape, 0) >= length
    for head in range(2):
        spare = lane == (1 - head) * DHEAD
        mark_ref[head] = jnp.where(spare & masked, MASKED, 0.0).astype(BF16)


GROUP = 2


def pair_lanes(pair):
    return slice(pair * 2 * DHEAD, (pair + 1) * 2 * DHEAD)


def attend(info, qkv, seqs, which, before):
    _, rows, width = qkv.shape
    span = rows // seqs
    pairs = width // (2 * DHEAD * GROUP)

    def body(info_ref, ins, held, rest):
        query_ref, key_ref, value_ref = ins[:3]
        mixed_ref, logsum_ref, mark_ref = rest

        @pl.when(pl.program_id(0) == 0)
        def _():
            fill_marks(mark_ref, info_ref[1 + which])

        own, spare = head_rows()

        def scores_of(pair, head):
            lanes = pair_lanes(pair)
            key_one = key_ref[0, :, lanes] * own[head] + mark_ref[head]
            return dot_nt(key_one, query_ref[0, :, lanes] * own[head] + spare[head])

        heads = [(pair, head) for pair in range(GROUP) for head in range(2)]
        ahead = [scores_of(*heads[0])]
        mixed = []
        for spot, (pair, head) in enumerate(heads):
            if spot + 1 < len(heads):
                ahead.append(scores_of(*heads[spot + 1]))
            scores = ahead[spot]
            top = jnp.max(scores, axis=0, keepdims=True)
            expo = jnp.exp(scores - top)
            total = jnp.sum(expo, axis=0, keepdims=True)
            if head == 0:
                value_t = value_ref[0, :, pair_lanes(pair)].T
            out = dot(value_t[head * DHEAD : (head + 1) * DHEAD], expo.astype(BF16))
            mixed.append(out / total)
            logsum_ref[0, 0, spot : spot + 1, :] = top + jnp.log(total)
            if head == 1:
                both = jnp.concatenate(mixed[-2:], axis=0)
                mixed_ref[:, pair_lanes(pair)] = both.T.astype(BF16)

    def block(part):
        return pl.BlockSpec((1, span, GROUP * 2 * DHEAD), lambda p, *_: (part, which, p))

    return call(
        body,
        (pairs,),
        info,
        (qkv, qkv, qkv) + before,
        [block(i) for i in range(3)] + [pl.BlockSpec(memory_space=pl.ANY)] * len(before),
        [],
        (shape_of((rows, width), BF16), shape_of((seqs, pairs, 8, span), F32)),
        (
            pl.BlockSpec((span, GROUP * 2 * DHEAD), lambda p, *_: (which, p)),
            pl.BlockSpec((1, 1, 8, span), lambda p, *_: (which, p, 0, 0)),
        ),
        [pltpu.VMEM((2, span, 2 * DHEAD), BF16)],
        8 * span * span * width,
        "attend",
        exps=span * span * HEADS,
        aliases={4: 0, 5: 1} if before else {},
    )


def attend_back(info, qkv, grad_mixed, logsum, seqs, which, steps):
    _, rows, width = qkv.shape
    span = rows // seqs
    pairs = width // (2 * DHEAD * GROUP)

    def body(info_ref, ins, held, rest):
        query_ref, key_ref, value_ref, grad_ref, logsum_ref = ins[:5]
        step_ref, sums_ref, mark_ref = rest

        @pl.when(pl.program_id(0) == 0)
        def _():
            fill_marks(mark_ref, info_ref[1 + which])

        own, spare = head_rows()

        def products_of(pair, head):
            lanes = pair_lanes(pair)
            key_one = key_ref[0, :, lanes] * own[head] + mark_ref[head]
            scores = dot_nt(key_one, query_ref[0, :, lanes] * own[head] + spare[head])
            return scores, dot_nt(value_ref[0, :, lanes] * own[head], grad_ref[:, lanes])

        heads = [(pair, head) for pair in range(GROUP) for head in range(2)]
        ahead = [products_of(*heads[0])]
        query_steps, key_steps, value_steps = [], [], []
        for spot, (pair, head) in enumerate(heads):
            if spot + 1 < len(heads):
                ahead.append(products_of(*heads[spot + 1]))
            scores, grad_probs = ahead[spot]
            lanes = pair_lanes(pair)
            probs = jnp.exp(scores - logsum_ref[0, 0, spot : spot + 1, :])
            value_steps.append(dot(probs.astype(BF16), grad_ref[:, lanes]))
            inner = jnp.sum(grad_probs * probs, axis=0, keepdims=True)
            grad_scores = (probs * (grad_probs - inner)).astype(BF16)
            key_steps.append(dot(grad_scores, query_ref[0, :, lanes]))
            if head == 0:
                key_t = key_ref[0, :, lanes].T
            query_steps.append(
                dot(key_t[head * DHEAD : (head + 1) * DHEAD], grad_scores) * SCALE
            )
            if head == 1:
                first = lax.broadcasted_iota(jnp.int32, (span, 2 * DHEAD), 1) < DHEAD
                query_step = jnp.concatenate(query_steps[-2:], axis=0).T.astype(BF16)
                value_step = jnp.where(first, *value_steps[-2:]).astype(BF16)
                step_ref[0, :, lanes] = query_step
                step_ref[1, :, lanes] = jnp.where(first, *key_steps[-2:]).astype(BF16)
                step_ref[2, :, lanes] = value_step
                for row, step in enumerate((query_step, value_step)):
                    sums_ref[row : row + 1, lanes] = jnp.sum(
                        step.astype(F32), axis=0, keepdims=True
                    )

    def block(part):
        return pl.BlockSpec((1, span, GROUP * 2 * DHEAD), lambda p, *_: (part, which, p))

    return call(
        body,
        (pairs,),
        info,
        (qkv, qkv, qkv, grad_mixed, logsum) + (() if steps is None else (steps,)),
        [block(i) for i in range(3)]
        + [
            pl.BlockSpec((span, GROUP * 2 * DHEAD), lambda p, *_: (which, p)),
            pl.BlockSpec((1, 1, 8, span), lambda p, *_: (which, p, 0, 0)),
        ]
        + ([] if steps is None else [pl.BlockSpec(memory_space=pl.ANY)]),
        [],
        (shape_of((3, rows, width), BF16), shape_of((8, width), F32)),
        (
            pl.BlockSpec((3, span, GROUP * 2 * DHEAD), lambda p, *_: (0, which, p)),
            pl.BlockSpec((8, GROUP * 2 * DHEAD), lambda p, *_: (0, p)),
        ),
        [pltpu.VMEM((2, span, 2 * DHEAD), BF16)],
        10 * span * span * width * 2,
        "attend_back",
        exps=span * span * HEADS,
        aliases={} if steps is None else {6: 0},
    )


def project_out(info, mixed, tokens, vectors, weight):
    rows, width = tokens.shape

    def body(info_ref, ins, held, rest):
        mixed_ref, tokens_ref, vector_ref = ins
        normed_ref, low_ref, factor_ref, matrix, sem = rest

        @pl.when(pl.program_id(0) == 0)
        def _():
            start_load(weight, held[0], matrix, info_ref[0], sem)
            wait_load(matrix, sem)

        for part in sub_blocks(TALL):
            branch = dot(mixed_ref[part, :], matrix[...]) + vector_ref[2:3, :]
            normed, factor = normalize(tokens_ref[part, :].astype(F32) + branch)
            normed_ref[part, :] = normed.astype(BF16)
            low_ref[part, :] = (normed * vector_ref[3:4, :] + vector_ref[4:5, :]).astype(BF16)
            factor_ref[part, :] = jnp.broadcast_to(factor, (SUB, 128))

    return call(
        body,
        (rows // TALL,),
        info,
        (mixed, tokens, vectors),
        (by_rows(width, TALL), by_rows(width, TALL), whole(vectors.shape)),
        [weight],
        (shape_of((rows, width), BF16), shape_of((rows, width), BF16), shape_of((rows, 128), F32)),
        (by_rows(width, TALL), by_rows(width, TALL), by_rows(128, TALL)),
        [pltpu.VMEM((width, width), BF16), pltpu.SemaphoreType.DMA],
        2 * rows * width * width,
        "project_out",
    )


def gelu_both(hidden):
    share = 0.5 * lax.erf(hidden * 0.7071067811865476) + 0.5
    bell = jnp.exp(-0.5 * (hidden * hidden))
    return hidden * share, share + hidden * (bell * 0.3989422804014327)


def feed_in(info, low, bias, weights, begin, end, before):
    rows, width = low.shape
    part = weights[0].columns
    wide = len(weights) * part
    steps = end - begin
    half = part // 2

    def body(info_ref, ins, held, rest):
        low_ref, bias_ref = ins[:2]
        active_ref, slope_ref, matrix, sem = rest
        step = pl.program_id(0)

        @pl.when(step == 0)
        def _():
            start_load(weights[begin], held[0], matrix.at[0], info_ref[0], sem.at[0])

        for i in range(steps):

            @pl.when(step == 2 * i)
            def _():
                wait_load(matrix.at[i], sem.at[i])

        for i in range(1, steps):

            @pl.when(step == 2 * i - 2)
            def _():
                start_load(weights[begin + i], held[i], matrix.at[i], info_ref[0], sem.at[i])

        for start in range(0, rows, BLOCK):
            some = pl.ds(start, BLOCK)
            columns = pl.ds(pl.multiple_of((step % 2) * half, half), half)
            hidden = dot(low_ref[some, :], matrix[step // 2, :, columns]) + bias_ref[...]
            active, slope = gelu_both(hidden)
            active_ref[some, :] = active.astype(BF16)
            slope_ref[some, :] = slope.astype(BF16)

    columns = pl.BlockSpec((rows, half), lambda i, *_: (0, 2 * begin + i))
    return call(
        body,
        (2 * steps,),
        info,
        (low, bias) + before,
        (whole(low.shape), pl.BlockSpec((1, half), lambda i, *_: (0, 2 * begin + i)))
        + (pl.BlockSpec(memory_space=pl.ANY),) * len(before),
        weights[begin:end],
        (shape_of((rows, wide), BF16), shape_of((rows, wide), BF16)),
        (columns, columns),
        [pltpu.VMEM((steps, width, part), BF16), pltpu.SemaphoreType.DMA((steps,))],
        2 * rows * width * part * steps,
        "feed_in",
        exps=rows * part * steps,
        aliases={3: 0, 4: 1} if before else {},
    )


def feed_out(info, active, normed, cotangent, vectors, weight, span):
    rows, wide = active.shape
    width = weight.columns
    chunks = chunks_of(weight)
    high = wide // chunks

    def body(info_ref, ins, held, rest):
        active_ref, normed_ref, cotangent_ref, vector_ref = ins
        out_ref, branch_ref, sums_ref, matrix, sem = rest
        step = pl.program_id(0)

        @pl.when(step == 0)
        def _():
            start_load(weight, held[0], matrix, info_ref[0], sem, chunks=chunks)
            sums_ref[...] = jnp.zeros_like(sums_ref)

        total = 0.0
        for i in range(chunks):
            some = slice(i * high, (i + 1) * high)

            @pl.when(step == 0)
            def _():
                wait_load(matrix.at[some], sem.at[i])

            total += dot(active_ref[:, some], matrix[some, :])
        sequence = (step * TALL) // span
        length = info_ref[1 + sequence]
        for part in sub_blocks(TALL):
            middle = normed_ref[part, :].astype(F32) * vector_ref[3:4, :] + vector_ref[4:5, :]
            branch = total[part, :] + vector_ref[5:6, :]
            second, factor = normalize(middle + branch)
            gain = vector_ref[6:7, :]
            out_ref[part, :] = (second * gain + vector_ref[7:8, :]).astype(BF16)
            places = step * TALL + part.start + lax.broadcasted_iota(jnp.int32, (SUB, 1), 0)
            valid = places - sequence * span < length
            grad = jnp.where(valid, cotangent_ref[part, :].astype(F32), 0.0)
            sums_ref[0:1, :] += jnp.sum(grad * second, axis=0, keepdims=True)
            sums_ref[1:2, :] += jnp.sum(grad, axis=0, keepdims=True)
            back = norm_back(grad * gain, second, factor)
            branch = back.astype(BF16)
            branch_ref[part, :] = branch
            sums_ref[2:3, :] += jnp.sum(branch.astype(F32), axis=0, keepdims=True)

    return call(
        body,
        (rows // TALL,),
        info,
        (active, normed, cotangent, vectors),
        (by_rows(wide, TALL), by_rows(width, TALL), by_rows(width, TALL), whole(vectors.shape)),
        [weight],
        (
            shape_of((rows, width), BF16),
            shape_of((rows, width), BF16),
            shape_of((8, width), F32),
        ),
        (by_rows(width, TALL), by_rows(width, TALL), whole((8, width))),
        [pltpu.VMEM((wide, width), BF16), pltpu.SemaphoreType.DMA((chunks,))],
        2 * rows * width * wide,
        "feed_out",
    )


def hidden_back(info, branch, slope, outer):
    rows, width = branch.shape
    wide = slope.shape[1]
    steps = chunks_of(outer)
    part = wide // steps

    def body(info_ref, ins, held, rest):
        branch_ref, slope_ref = ins
        hidden_ref, bias_ref, big, sem = rest
        step = pl.program_id(0)

        @pl.when(step == 0)
        def _():
            start_load(outer, held[0], big, info_ref[0], sem, chunks=steps)

        some = pl.ds(pl.multiple_of(step * part, part), part)
        wait_load(big.at[some], sem.at[step])
        total = jnp.zeros((8, part), F32)
        for start in range(0, rows, BLOCK):
            here = slice(start, start + BLOCK)
            grad = dot_nt(branch_ref[here, :], big[some, :]) * slope_ref[here, :].astype(F32)
            grad = grad.astype(BF16)
            hidden_ref[here, :] = grad
            total += jnp.sum(grad.astype(F32).reshape(BLOCK // 8, 8, part), axis=0)
        bias_ref[...] = jnp.broadcast_to(jnp.sum(total, axis=0, keepdims=True), bias_ref.shape)

    columns = pl.BlockSpec((rows, part), lambda i, *_: (0, i))
    return call(
        body,
        (steps,),
        info,
        (branch, slope),
        (whole(branch.shape), columns),
        [outer],
        (shape_of((rows, wide), BF16), shape_of((8, wide), F32)),
        (columns, pl.BlockSpec((8, part), lambda i, *_: (0, i))),
        [pltpu.VMEM((wide, width), BF16), pltpu.SemaphoreType.DMA((steps,))],
        2 * rows * width * wide,
        "hidden_back",
    )


def middle_back(info, branch, hidden, normed, factor, vectors, inner, attn):
    rows, width = branch.shape
    wide = hidden.shape[1]
    chunks, part = len(inner), inner[0].columns

    def body(info_ref, ins, held, rest):
        branch_ref, hidden_ref, normed_ref, factor_ref, vector_ref = ins
        proj_ref, mixed_ref, sums_ref, big, small, sem = rest
        step = pl.program_id(0)

        @pl.when(step == 0)
        def _():
            for i in range(chunks):
                start_load(inner[i], held[i], big.at[i], info_ref[0], sem.at[i])
            start_load(attn, held[chunks], small, info_ref[0], sem.at[chunks])
            sums_ref[...] = jnp.zeros_like(sums_ref)

        middle = branch_ref[...].astype(F32)
        for i in range(chunks):

            @pl.when(step == 0)
            def _():
                wait_load(big.at[i], sem.at[i])

            middle += dot_nt(hidden_ref[:, i * part : (i + 1) * part], big[i])

        @pl.when(step == 0)
        def _():
            wait_load(small, sem.at[chunks])

        normed = normed_ref[...].astype(F32)
        sums_ref[0:1, :] += jnp.sum(middle * normed, axis=0, keepdims=True)
        sums_ref[1:2, :] += jnp.sum(middle, axis=0, keepdims=True)
        first = norm_back(middle * vector_ref[3:4, :], normed, factor_ref[:, 0:1])
        proj = first.astype(BF16)
        proj_ref[...] = proj
        sums_ref[2:3, :] += jnp.sum(proj.astype(F32), axis=0, keepdims=True)
        mixed_ref[...] = dot_nt(proj, small[...]).astype(BF16)

    return call(
        body,
        (rows // BLOCK,),
        info,
        (branch, hidden, normed, factor, vectors),
        (by_rows(width), by_rows(wide), by_rows(width), by_rows(128), whole(vectors.shape)),
        inner + [attn],
        (shape_of((rows, width), BF16), shape_of((rows, width), BF16), shape_of((8, width), F32)),
        (by_rows(width), by_rows(width), whole((8, width))),
        [
            pltpu.VMEM((chunks, width, part), BF16),
            pltpu.VMEM((width, width), BF16),
            pltpu.SemaphoreType.DMA((chunks + 1,)),
        ],
        2 * rows * width * wide + 2 * rows * width * width,
        "middle_back",
    )


def input_back(info, proj, steps, weights):
    rows, width = proj.shape

    def body(info_ref, ins, held, rest):
        proj_ref, step_ref = ins
        out_ref, matrix, sem = rest

        @pl.when(pl.program_id(0) == 0)
        def _():
            for i, weight in enumerate(weights):
                start_load(weight, held[i], matrix.at[i], info_ref[0], sem.at[i])

        total = proj_ref[...].astype(F32)
        for i in range(3):

            @pl.when(pl.program_id(0) == 0)
            def _():
                wait_load(matrix.at[i], sem.at[i])

            total += dot_nt(step_ref[i], matrix[i])
        out_ref[...] = total.astype(BF16)

    return call(
        body,
        (rows // BLOCK,),
        info,
        (proj, steps),
        (by_rows(width), pl.BlockSpec((3, BLOCK, width), lambda i, *_: (0, i, 0))),
        weights,
        shape_of((rows, width), BF16),
        by_rows(width),
        [pltpu.VMEM((3, width, width), BF16), pltpu.SemaphoreType.DMA((3,))],
        6 * rows * width * width,
        "input_back",
    )


def weight_grad(info, lefts, rights, places, name):
    rows, height = lefts[0].shape
    slot = height // (8 * places)
    block = 8 * slot
    part = min(1024, rights[0].shape[-1])
    counts = [r.shape[0] if r.ndim == 3 else r.shape[1] // part for r in rights]
    firsts = [sum(counts[:i]) for i in range(len(counts))]
    parts = sum(counts)
    half = height // 2

    def body(info_ref, ins, held, rest):
        left_refs, right_refs = ins[: len(lefts)], ins[len(lefts) :]
        keep_ref, send_ref, sorted_ref = rest
        here = info_ref[0]
        step = pl.program_id(0)
        for left_ref, right_ref, first, count in zip(left_refs, right_refs, firsts, counts):

            @pl.when(step == first)
            def _():
                for z in range(places):
                    turned = left_ref[:, z * block : (z + 1) * block].T
                    for k in range(8):
                        relative = (z * 8 + k) ^ here
                        spot = (relative & 1) * 4 + ((relative >> 1) & 3)
                        spot = spot * places + (relative >> 3)
                        sorted_ref[pl.ds(pl.multiple_of(spot * slot, slot), slot), :] = turned[
                            k * slot : (k + 1) * slot
                        ]

            @pl.when((step >= first) & (step < first + count))
            def _():
                right = right_ref[0] if len(right_ref.shape) == 3 else right_ref[...]
                for out_ref, start in ((keep_ref, 0), (send_ref, half)):
                    for side in range(4):
                        size = half // 4
                        total = dot(sorted_ref[start + side * size : start + (side + 1) * size, :], right)
                        out_ref[side] = total.astype(BF16).reshape(places, slot, part)

    def right_spec(right, first, count):
        place = lambda w: jnp.clip(w - first, 0, count - 1)
        if right.ndim == 3:
            return pl.BlockSpec((1, rows, part), lambda w, *_: (place(w), 0, 0))
        return pl.BlockSpec((rows, part), lambda w, *_: (0, place(w)))

    out = shape_of((4, places, parts * slot, part), BF16)
    out_block = pl.BlockSpec((4, places, slot, part), lambda w, *_: (0, 0, w, 0))
    return call(
        body,
        (parts,),
        info,
        tuple(lefts) + tuple(rights),
        [whole(left.shape) for left in lefts]
        + [right_spec(r, f, c) for r, f, c in zip(rights, firsts, counts)],
        [],
        (out, out),
        (out_block, out_block),
        [pltpu.VMEM((height, rows), BF16)],
        2 * rows * height * parts * part,
        name,
    )


def weight_grad_tall(info, left, right, places, name):
    rows, height = left.shape
    width = right.shape[1]
    slot = height // (8 * places)

    def body(info_ref, ins, held, rest):
        left_ref, right_ref = ins
        keep_ref, send_ref = rest
        here = info_ref[0]
        for side in range(4):
            for out_ref, other in ((keep_ref, 0), (send_ref, 1)):
                which = (here & 7) ^ (2 * side + other)
                some = pl.ds(pl.multiple_of(which * slot, slot), slot)
                out_ref[side, 0] = dot_tn(left_ref[:, some], right_ref[...]).astype(BF16)

    out = shape_of((4, places, slot, width), BF16)
    block = pl.BlockSpec((4, 1, slot, width), lambda z, *_: (0, z, 0, 0))
    return call(
        body,
        (places,),
        info,
        (left, right),
        (
            pl.BlockSpec((rows, 8 * slot), lambda z, info: (0, z ^ (info[0] >> 3))),
            whole(right.shape),
        ),
        [],
        (out, out),
        (block, block),
        [],
        2 * rows * height * width,
        name,
    )


def sums_of(second, first, attn, wide):
    attn = sum(attn)[:2]
    return jnp.concatenate([second[:3], first[:3], attn, wide[:1].reshape(-1, second.shape[1])])


def per_device(
    tokens,
    lengths,
    cotangent,
    query_weight,
    query_bias,
    key_weight,
    value_weight,
    value_bias,
    attn_weight,
    attn_bias,
    first_gain,
    first_shift,
    inner_weight,
    inner_bias,
    outer_weight,
    outer_bias,
    second_gain,
    second_shift,
):
    n = lax.axis_size("fsdp")
    here = lax.axis_index("fsdp").astype(jnp.int32)
    seqs = lengths.shape[0]
    rows, width = tokens.shape
    wide = inner_weight.shape[1]
    span = rows // seqs
    own = query_weight.shape[0]
    tall = outer_weight.shape[0]
    staged = n in (16, 32) and own % 16 == 0
    info = jnp.concatenate([here[None], lengths])

    full = lambda w: lax.all_gather(w, "fsdp", axis=0, tiled=True)
    whole_weight = lambda w: Weight((w,), 0, 0, w.shape[0] // n, w.shape[0], w.shape[1])

    small = jnp.stack(
        (
            query_bias,
            value_bias,
            attn_bias,
            first_gain,
            first_shift,
            outer_bias,
            second_gain,
            second_shift,
        )
    )
    table = jnp.zeros((8 + wide // width, width), BF16)
    table = lax.dynamic_update_slice(table, small, (0, here * own))
    spot = here * tall
    table = lax.dynamic_update_slice(table, inner_bias[None], (8 + spot // width, spot % width))

    if staged:
        places = n // 8
        one = stacked([query_weight, key_weight, value_weight], width)
        two = stacked([inner_weight, attn_weight], width)
        others = gather_line(one)
        for bits in (1, 2, 4):
            table = sum_round(table, (bits,))
        table, two, *others = hold(table, two, *others)
        line = jnp.concatenate([one, *others])
        beside, above = gather_sides(line)
        cut = 3 * own
        others_top = gather_line(two[:cut])
        line, beside, above, two, *others_top = hold(line, beside, above, two, *others_top)
        others_low = gather_line(two[cut:])
        near = (line, beside, above) + gather_across(beside, above)
        table, two, *near = hold(table, two, *near, *others_low)
        near, others_low = near[:5], near[5:]
        table = sum_round(table, [8 * k for k in range(1, places)])
        pieces = near + [flip(piece, 1) for piece in near]
        line_two = jnp.concatenate([two] + [p for pair in zip(others_top, others_low) for p in pair])
        table, line_two, three, *pieces = hold(table, line_two, outer_weight, *pieces)
        qkv_weights = [Weight(pieces, 3 * own, i * own, own, width, width) for i in range(3)]
    else:
        table = sum_everywhere(table)
        qkv_weights = [whole_weight(full(w)) for w in (query_weight, key_weight, value_weight)]
        outer = whole_weight(full(outer_weight))
    table = table.astype(F32)
    vectors, wide_bias = table[:8], table[8:].reshape(1, wide)
    biases = jnp.stack([vectors[0:1], jnp.zeros((1, width), F32), vectors[1:2]])

    blocks = wide // width
    if staged:
        beside, above = gather_sides(line_two)
        others_three = gather_line(three)
        qkv = project_qkv(info, tokens, biases, qkv_weights)
        result = attend(info, qkv, seqs, 0, ())
        beside, above, *result = hold(beside, above, *others_three, *result)
        others_three, result = result[: places - 1], result[places - 1 :]
        near = (line_two, beside, above) + gather_across(beside, above)
        far = tuple(flip(piece, 1) for piece in near[:3])
        line_three = jnp.concatenate([three, *others_three])
        for which in range(1, seqs):
            result = attend(info, qkv, seqs, which, tuple(result))
        mixed, logsum, line_three, *pieces = hold(*result, line_three, *near, *far)
        beside, above = gather_sides(line_three)
        pieces = pieces + [flip(piece, 1) for piece in pieces[3:5]]
        inner = [Weight(pieces, 5 * own, i * own, own, width, width) for i in range(blocks)]
        attn = Weight(pieces, 5 * own, blocks * own, own, width, width)
        normed, low, factor = project_out(info, mixed, tokens, vectors, attn)
        active, slope = feed_in(info, low, wide_bias, inner, 0, blocks // 2, ())
        line_three, beside, above, active, slope = hold(line_three, beside, above, active, slope)
        near = (line_three, beside, above) + gather_across(beside, above)
        far = tuple(flip(piece, 1) for piece in near[:3])
        active, slope = feed_in(info, low, wide_bias, inner, blocks // 2, blocks, (active, slope))
        active, *pieces = hold(active, *near, *far)
        pieces = pieces + [flip(piece, 1) for piece in pieces[3:5]]
        outer = Weight(pieces, tall, 0, tall, wide, width)
    else:
        attn, inner = whole_weight(full(attn_weight)), full(inner_weight)
        inner = [Weight((inner,), 0, 0, own, width, width, i * width) for i in range(blocks)]
        qkv = project_qkv(info, tokens, biases, qkv_weights)
        result = ()
        for which in range(seqs):
            result = attend(info, qkv, seqs, which, tuple(result))
        mixed, logsum = result
        normed, low, factor = project_out(info, mixed, tokens, vectors, attn)
        active, slope = feed_in(info, low, wide_bias, inner, 0, blocks, ())
    output, branch, sums_second = feed_out(
        info, active, normed, cotangent, vectors, outer, span
    )

    def back_of(hidden):
        return middle_back(info, branch, hidden, normed, factor, vectors, inner, attn)

    def attend_all(grad_mixed):
        steps, sums = None, []
        for which in range(seqs):
            steps, some = attend_back(info, qkv, grad_mixed, logsum, seqs, which, steps)
            sums.append(some)
        return steps, sums

    if staged:
        keep_o, send_o = weight_grad_tall(info, active, branch, places, "grad_outer")
        keep_o, send_o, branch = hold(keep_o, send_o, branch)
        got_o = flip(send_o, 1)
        grad_hidden, sums_wide = hidden_back(info, branch, slope, outer)
        got_o, grad_hidden, sums_wide = hold(got_o, grad_hidden, sums_wide)
        sides_o = sides_of(keep_o, got_o)
        grad_hidden, *sides_o = hold(grad_hidden, *sides_o)
        first_o = flip_first(sides_o)
        grad_proj, grad_mixed, sums_first = back_of(grad_hidden)
        first_o, grad_proj, grad_mixed, sums_first = hold(
            first_o, grad_proj, grad_mixed, sums_first
        )
        second_o = flip_second(sides_o, first_o)
        keep, send = weight_grad(
            info, (low, mixed), (grad_hidden, grad_proj), places, "grad_inner_attn"
        )
        second_o, keep, send, grad_mixed = hold(second_o, keep, send, grad_mixed)
        got = flip(send, 1)
        kept_o, arrived_o = flip_line(keep_o, got_o, first_o, second_o)
        steps, some = attend_back(info, qkv, grad_mixed, logsum, seqs, 0, None)
        sums_attn = [some]
        got, kept_o, arrived_o, steps = hold(got, kept_o, arrived_o, steps)
        sides = sides_of(keep, got)
        outer_wgrad = add_low(kept_o, *arrived_o)
        steps, outer_wgrad, *sides = hold(steps, outer_wgrad, *sides)
        first = flip_first(sides)
        for which in range(1, seqs):
            steps, some = attend_back(info, qkv, grad_mixed, logsum, seqs, which, steps)
            sums_attn.append(some)
        keep_two, send_two = weight_grad(info, (tokens,), (steps,), places, "grad_qkv")
        first, steps, keep_two, send_two, *sums_attn = hold(
            first, steps, keep_two, send_two, *sums_attn
        )
        got_two = flip(send_two, 1)
        sums = sums_of(sums_second, sums_first, sums_attn, sums_wide)
        sums = sum_round(sums, (1,))
        second = flip_second(sides, first)
        input_grad = input_back(info, grad_proj, steps, qkv_weights)
        got_two, sums, second, input_grad = hold(got_two, sums, second, input_grad)
        moved_two = flip_diagonal(keep_two, got_two)
        sums = sum_round(sums, [8 * k for k in range(1, places)])
        sums, keep, *moved_two = hold(sums, keep, *moved_two)
        first_two, second_two = flip_whole(keep_two, got_two, moved_two)
        kept, arrived = flip_line(keep, got, first, second)
        sums, first_two, second_two = hold(sums, first_two, second_two)
        sums = sum_round(sum_round(sums, (2,)), (4,))
        kept_two, arrived_two = flip_line(keep_two, got_two, first_two, second_two)
        sums, kept, arrived = hold(sums, kept, arrived)
        both = add_low(kept, *arrived)
        qkv_wgrad = add_low(kept_two, *arrived_two)
        attn_wgrad = both[wide // width * own :]
        inner_wgrad = both[: wide // width * own].reshape(wide // width, own, width)
        inner_wgrad = inner_wgrad.transpose(1, 0, 2).reshape(own, wide)
    else:
        scatter = lambda g: lax.psum_scatter(g, "fsdp", scatter_dimension=0, tiled=True)
        outer_wgrad = scatter(dot_tn(active, branch))
        grad_hidden, sums_wide = hidden_back(info, branch, slope, outer)
        grad_proj, grad_mixed, sums_first = back_of(grad_hidden)
        steps, sums_attn = attend_all(grad_mixed)
        input_grad = input_back(info, grad_proj, steps, qkv_weights)
        inner_wgrad = scatter(dot_tn(low, grad_hidden))
        attn_wgrad = scatter(dot_tn(mixed, grad_proj))
        qkv_wgrad = jnp.concatenate([scatter(dot_tn(tokens, steps[i])) for i in range(3)])
        sums = sum_everywhere(sums_of(sums_second, sums_first, sums_attn, sums_wide))

    mine = lax.dynamic_slice(sums, (0, here * own), (8, own))
    inner_bgrad = lax.dynamic_slice(sums, (8 + spot // width, spot % width), (1, tall))[0]
    return (
        output,
        input_grad,
        qkv_wgrad[:own],
        mine[6],
        qkv_wgrad[own : 2 * own],
        qkv_wgrad[2 * own :],
        mine[7],
        attn_wgrad,
        mine[5],
        mine[3],
        mine[4],
        inner_wgrad,
        inner_bgrad,
        outer_wgrad,
        mine[2],
        mine[0],
        mine[1],
    )


def solution(mesh):
    rows, vector = P("fsdp", None), P("fsdp")
    return jax.shard_map(
        per_device,
        mesh=mesh,
        in_specs=(
            rows,
            vector,
            rows,
            rows,
            vector,
            rows,
            rows,
            vector,
            rows,
            vector,
            vector,
            vector,
            rows,
            vector,
            rows,
            vector,
            vector,
            vector,
        ),
        out_specs=(
            rows,
            rows,
            rows,
            vector,
            rows,
            rows,
            vector,
            rows,
            vector,
            vector,
            vector,
            rows,
            vector,
            rows,
            vector,
            vector,
            vector,
        ),
        check_vma=False,
    )
```

```python
import math

import jax
import jax.numpy as jnp
from jax import lax
from jax.experimental import pallas as pl
from jax.experimental.pallas import tpu as pltpu
from jax.sharding import PartitionSpec as P

HEADS = 16
DHEAD = 64
EPSILON = 1e-05
MASKED = -1e30
SCALE = DHEAD ** (-0.5)
F32 = jnp.float32
BF16 = jnp.bfloat16
BLOCK = 256
TALL = 256
SUB = 128
FI = 512
HB = 512
SPARE = 10 * 1024 * 1024
ROOM = 60 * 1024 * 1024
PIECES = pltpu.HBM
TIGHT = ("attend_back", "grad_qkv")
SIDES = (0, 2, 4, 6)


def dot(left, right):
    return jnp.dot(left, right, preferred_element_type=F32)


def dot_nt(left, right):
    return lax.dot_general(left, right, (((1,), (1,)), ((), ())), preferred_element_type=F32)


def dot_tn(left, right):
    return lax.dot_general(left, right, (((0,), (0,)), ((), ())), preferred_element_type=F32)


def normalize(rows):
    centred = rows - jnp.mean(rows, axis=-1, keepdims=True)
    factor = lax.rsqrt(jnp.mean(centred * centred, axis=-1, keepdims=True) + EPSILON)
    return centred * factor, factor


def norm_back(grad, normed, factor):
    mean_one = jnp.mean(grad, axis=-1, keepdims=True)
    mean_two = jnp.mean(grad * normed, axis=-1, keepdims=True)
    return factor * (grad - mean_one - normed * mean_two)


def flip(array, bits):
    n = lax.axis_size("fsdp")
    return lax.ppermute(array, "fsdp", [(i, i ^ bits) for i in range(n)])


def hold(*values):
    return lax.optimization_barrier(values)


class Weight:
    def __init__(self, pieces, slot, offset, count, rows, columns, first=0):
        self.pieces, self.slot, self.offset, self.count = pieces, slot, offset, count
        self.rows, self.columns, self.first = rows, columns, first


def gather_line(shard):
    n = lax.axis_size("fsdp")
    return [flip(shard, 8 * k) for k in range(1, n // 8)]


def gather_sides(line):
    return flip(line, 2), flip(line, 4)


def gather_across(beside, above):
    half = beside.shape[0] // 2
    return flip(above[:half], 2), flip(beside[half:], 4)


def start_load(weight, refs, target, here, sem, chunks=0):
    if len(refs) == 1:
        tall = weight.rows // max(chunks, 1)
        columns = pl.ds(weight.first, weight.columns)
        for i in range(max(chunks, 1)):
            some = pl.ds(i * tall, tall)
            pltpu.make_async_copy(
                refs[0].at[some, columns], target.at[some], sem.at[i] if chunks else sem
            ).start()
        return
    count = weight.count
    places = weight.rows // count // 8
    spots = [(side, range(places)) for side in SIDES[:3]]
    spots += [(SIDES[3], range(places // 2)), (SIDES[3], range(places // 2, places))]
    spots += [(side ^ 1, which) for side, which in spots]
    for (low, which), ref in zip(spots, refs):
        for position, k in enumerate(which):
            owner = here ^ (low ^ (8 * k))
            pltpu.make_async_copy(
                ref.at[pl.ds(position * weight.slot + weight.offset, count)],
                target.at[pl.ds(pl.multiple_of(owner * count, count), count)],
                sem.at[(owner >> 3) * chunks // places] if chunks else sem,
            ).start()


def chunks_of(weight):
    return 4 if len(weight.pieces) == 1 else weight.rows // weight.count // 8


def wait_load(target, sem):
    pltpu.make_async_copy(target, target, sem).wait()


def sum_everywhere(array):
    n = lax.axis_size("fsdp")
    bit = 1
    while bit < n:
        array = array + flip(array, bit)
        bit *= 2
    return array


def sum_round(array, flips):
    return sum([flip(array, bits) for bits in flips], array)


def add_low(*arrays):
    total = arrays[0].astype(F32)
    for array in arrays[1:]:
        total = total + array.astype(F32)
    return total


def low_sum(*arrays):
    return add_low(*arrays).astype(BF16)


def sides_of(keep, got):
    half = max(keep.shape[1] // 2, 1)
    parts = ((3, 0), (3, half), (1, 0), (2, half), (1, half), (2, 0))
    return [low_sum(keep[s, p : p + half], got[s, p : p + half]) for s, p in parts]


def flip_first(sides):
    return flip(sides[0], 2), flip(sides[1], 4), flip(sides[2], 2), flip(sides[3], 4)


def flip_second(sides, first):
    return flip(low_sum(sides[4], first[1]), 2), flip(low_sum(sides[5], first[0]), 4)


def flip_diagonal(keep, got):
    half = max(keep.shape[1] // 2, 1)
    low = lambda p: low_sum(keep[3, p : p + half], got[3, p : p + half])
    return flip(low(0), 2), flip(low(half), 4)


def flip_whole(keep, got, moved):
    half = max(keep.shape[1] // 2, 1)
    beside = [low_sum(keep[1, :half], got[1, :half]), low_sum(keep[1, half:], got[1, half:], moved[1])]
    above = [low_sum(keep[2, :half], got[2, :half], moved[0]), low_sum(keep[2, half:], got[2, half:])]
    beside, above = flip(jnp.concatenate(beside), 2), flip(jnp.concatenate(above), 4)
    return (None, None, beside[:half], above[half:]), (beside[half:], above[:half])


def flip_line(keep, got, first, second):
    places = keep.shape[1]
    half = max(places // 2, 1)
    pieces = []
    for k in range(places):
        pair = (first[2][k], second[1][k]) if k < half else (second[0][k - half], first[3][k - half])
        pieces.append(add_low(keep[0, k], got[0, k], *pair))
    arrived = [flip(pieces[k].astype(BF16), 8 * k) for k in range(1, places)]
    return pieces[0], arrived


def operands_of(weights):
    arrays, where = [], []
    for weight in weights:
        places = []
        for piece in weight.pieces:
            for position, array in enumerate(arrays):
                if array is piece:
                    places.append(position)
                    break
            else:
                places.append(len(arrays))
                arrays.append(piece)
        where.append(places)
    return arrays, where


def call(body, grid, info, inputs, specs, weights, outs, out_specs, scratch, flops, name, exps=0, aliases={}):
    arrays, where = operands_of(weights)
    count = len(inputs)

    def kernel(info_ref, *refs):
        ins = refs[:count]
        pieces = refs[count : count + len(arrays)]
        held = [[pieces[p] for p in places] for places in where]
        body(info_ref, ins, held, refs[count + len(arrays) :])

    room = SPARE
    flat = list(zip(specs, inputs)) + list(zip(jax.tree.leaves(out_specs), jax.tree.leaves(outs)))
    for spec, array in flat:
        if spec.block_shape is not None:
            room += 2 * math.prod(spec.block_shape) * array.dtype.itemsize
    for held in scratch:
        if getattr(held, "shape", None) and held.dtype in (F32, BF16):
            room += math.prod(held.shape) * held.dtype.itemsize
    moved = sum(a.size * a.dtype.itemsize for a in list(inputs) + arrays)
    moved += sum(o.size * o.dtype.itemsize for o in jax.tree.leaves(outs))
    return pl.pallas_call(
        kernel,
        grid_spec=pltpu.PrefetchScalarGridSpec(
            num_scalar_prefetch=1,
            grid=grid,
            in_specs=list(specs) + [pl.BlockSpec(memory_space=PIECES)] * len(arrays),
            out_specs=out_specs,
            scratch_shapes=scratch,
        ),
        out_shape=outs,
        compiler_params=pltpu.CompilerParams(
            vmem_limit_bytes=room if name in TIGHT else ROOM, dimension_semantics=("arbitrary",) * len(grid)
        ),
        cost_estimate=pl.CostEstimate(flops=flops, bytes_accessed=moved, transcendentals=exps),
        input_output_aliases=aliases,
        name=name,
    )(info, *inputs, *arrays)


def shape_of(shape, dtype):
    return jax.ShapeDtypeStruct(shape, dtype)


def whole(shape):
    return pl.BlockSpec(shape, lambda *_: (0,) * len(shape))


def ahead_of(product_of, rows, size):
    blocks = [slice(start, start + size) for start in range(0, rows, size)]
    coming = product_of(blocks[0])
    for spot, block in enumerate(blocks):
        product = coming
        if spot + 1 < len(blocks):
            coming = product_of(blocks[spot + 1])
        yield block, product


def sub_blocks(rows):
    return [slice(start, start + SUB) for start in range(0, rows, SUB)]


def by_rows(columns, rows=BLOCK):
    return pl.BlockSpec((rows, columns), lambda i, *_: (i, 0))


def stacked(arrays, columns):
    rows = [array.shape[0] for array in arrays for _ in range(array.shape[1] // columns)]

    def kernel(*refs):
        out_ref, start = refs[-1], 0
        for ref in refs[:-1]:
            for first in range(0, ref.shape[1], columns):
                out_ref[start : start + ref.shape[0], :] = ref[:, first : first + columns]
                start += ref.shape[0]

    return pl.pallas_call(
        kernel,
        out_shape=shape_of((sum(rows), columns), arrays[0].dtype),
        name="stacked",
    )(*arrays)


def project_qkv(info, tokens, biases, weights):
    rows, width = tokens.shape

    def body(info_ref, ins, held, rest):
        tokens_ref, bias_ref = ins
        out_ref, matrix, sem = rest
        which = pl.program_id(0)

        @pl.when(which == 0)
        def _():
            start_load(weights[0], held[0], matrix.at[0], info_ref[0], sem.at[0])

        wait_load(matrix.at[which], sem.at[which])
        for i in range(1, 3):

            @pl.when(which == i - 1)
            def _():
                start_load(weights[i], held[i], matrix.at[i], info_ref[0], sem.at[i])

        factor = jnp.where(which == 0, SCALE, 1.0).astype(F32)
        for start in range(0, rows, BLOCK):
            part = pl.ds(start, BLOCK)
            total = dot(tokens_ref[part, :], matrix[which]) + bias_ref[0]
            out_ref[0, part, :] = (total * factor).astype(BF16)

    return call(
        body,
        (3,),
        info,
        (tokens, biases),
        (whole(tokens.shape), pl.BlockSpec((1, 1, width), lambda i, *_: (i, 0, 0))),
        weights,
        shape_of((3, rows, width), BF16),
        pl.BlockSpec((1, rows, width), lambda i, *_: (i, 0, 0)),
        [pltpu.VMEM((3, width, width), BF16), pltpu.SemaphoreType.DMA((3,))],
        6 * rows * width * width,
        "project_qkv",
    )


def head_rows():
    lane = lax.broadcasted_iota(jnp.int32, (1, 2 * DHEAD), 1)
    own = [(lane // DHEAD == head).astype(F32).astype(BF16) for head in range(2)]
    spare = [(lane == (1 - head) * DHEAD).astype(F32).astype(BF16) for head in range(2)]
    return own, spare


def fill_marks(mark_ref, length):
    shape = mark_ref.shape[1:]
    lane = lax.broadcasted_iota(jnp.int32, shape, 1)
    masked = lax.broadcasted_iota(jnp.int32, shape, 0) >= length
    for head in range(2):
        spare = lane == (1 - head) * DHEAD
        mark_ref[head] = jnp.where(spare & masked, MASKED, 0.0).astype(BF16)


GROUP = 4


def pair_lanes(pair):
    return slice(pair * 2 * DHEAD, (pair + 1) * 2 * DHEAD)


def attend(info, qkv, seqs, which, before):
    _, rows, width = qkv.shape
    span = rows // seqs
    pairs = width // (2 * DHEAD * GROUP)

    def body(info_ref, ins, held, rest):
        query_ref, key_ref, value_ref = ins[:3]
        mixed_ref, logsum_ref, mark_ref = rest

        @pl.when(pl.program_id(0) == 0)
        def _():
            fill_marks(mark_ref, info_ref[1 + which])

        own, spare = head_rows()

        def scores_of(pair, head):
            lanes = pair_lanes(pair)
            key_one = key_ref[0, :, lanes] * own[head] + mark_ref[head]
            return dot_nt(key_one, query_ref[0, :, lanes] * own[head] + spare[head])

        heads = [(pair, head) for pair in range(GROUP) for head in range(2)]
        ahead = [scores_of(*heads[0])]
        mixed = []
        for spot, (pair, head) in enumerate(heads):
            if spot + 1 < len(heads):
                ahead.append(scores_of(*heads[spot + 1]))
            scores = ahead[spot]
            top = jnp.max(scores, axis=0, keepdims=True)
            expo = jnp.exp(scores - top)
            total = jnp.sum(expo, axis=0, keepdims=True)
            if head == 0:
                value_t = value_ref[0, :, pair_lanes(pair)].T
            out = dot(value_t[head * DHEAD : (head + 1) * DHEAD], expo.astype(BF16))
            mixed.append(out / total)
            logsum_ref[0, 0, spot : spot + 1, :] = top + jnp.log(total)
            if head == 1:
                both = jnp.concatenate(mixed[-2:], axis=0)
                mixed_ref[:, pair_lanes(pair)] = both.T.astype(BF16)

    def block(part):
        return pl.BlockSpec((1, span, GROUP * 2 * DHEAD), lambda p, *_: (part, which, p))

    return call(
        body,
        (pairs,),
        info,
        (qkv, qkv, qkv) + before,
        [block(i) for i in range(3)] + [pl.BlockSpec(memory_space=pl.ANY)] * len(before),
        [],
        (shape_of((rows, width), BF16), shape_of((seqs, pairs, 8, span), F32)),
        (
            pl.BlockSpec((span, GROUP * 2 * DHEAD), lambda p, *_: (which, p)),
            pl.BlockSpec((1, 1, 8, span), lambda p, *_: (which, p, 0, 0)),
        ),
        [pltpu.VMEM((2, span, 2 * DHEAD), BF16)],
        8 * span * span * width,
        "attend",
        exps=span * span * HEADS,
        aliases={4: 0, 5: 1} if before else {},
    )


def attend_back(info, qkv, grad_mixed, logsum, seqs, which, steps):
    _, rows, width = qkv.shape
    span = rows // seqs
    pairs = width // (2 * DHEAD * GROUP)

    def body(info_ref, ins, held, rest):
        query_ref, key_ref, value_ref, grad_ref, logsum_ref = ins[:5]
        step_ref, sums_ref, mark_ref = rest

        @pl.when(pl.program_id(0) == 0)
        def _():
            fill_marks(mark_ref, info_ref[1 + which])

        own, spare = head_rows()

        def products_of(pair, head):
            lanes = pair_lanes(pair)
            key_one = key_ref[0, :, lanes] * own[head] + mark_ref[head]
            scores = dot_nt(key_one, query_ref[0, :, lanes] * own[head] + spare[head])
            return scores, dot_nt(value_ref[0, :, lanes] * own[head], grad_ref[:, lanes])

        heads = [(pair, head) for pair in range(GROUP) for head in range(2)]
        ahead = [products_of(*heads[0])]
        query_steps, key_steps, value_steps = [], [], []
        for spot, (pair, head) in enumerate(heads):
            if spot + 1 < len(heads):
                ahead.append(products_of(*heads[spot + 1]))
            scores, grad_probs = ahead[spot]
            lanes = pair_lanes(pair)
            probs = jnp.exp(scores - logsum_ref[0, 0, spot : spot + 1, :])
            value_steps.append(dot(probs.astype(BF16), grad_ref[:, lanes]))
            inner = jnp.sum(grad_probs * probs, axis=0, keepdims=True)
            grad_scores = (probs * (grad_probs - inner)).astype(BF16)
            key_steps.append(dot(grad_scores, query_ref[0, :, lanes]))
            if head == 0:
                key_t = key_ref[0, :, lanes].T
            query_steps.append(
                dot(key_t[head * DHEAD : (head + 1) * DHEAD], grad_scores) * SCALE
            )
            if head == 1:
                first = lax.broadcasted_iota(jnp.int32, (span, 2 * DHEAD), 1) < DHEAD
                query_step = jnp.concatenate(query_steps[-2:], axis=0).T.astype(BF16)
                value_step = jnp.where(first, *value_steps[-2:]).astype(BF16)
                step_ref[0, :, lanes] = query_step
                step_ref[1, :, lanes] = jnp.where(first, *key_steps[-2:]).astype(BF16)
                step_ref[2, :, lanes] = value_step
                for row, step in enumerate((query_step, value_step)):
                    sums_ref[row : row + 1, lanes] = jnp.sum(
                        step.astype(F32), axis=0, keepdims=True
                    )

    def block(part):
        return pl.BlockSpec((1, span, GROUP * 2 * DHEAD), lambda p, *_: (part, which, p))

    return call(
        body,
        (pairs,),
        info,
        (qkv, qkv, qkv, grad_mixed, logsum) + (() if steps is None else (steps,)),
        [block(i) for i in range(3)]
        + [
            pl.BlockSpec((span, GROUP * 2 * DHEAD), lambda p, *_: (which, p)),
            pl.BlockSpec((1, 1, 8, span), lambda p, *_: (which, p, 0, 0)),
        ]
        + ([] if steps is None else [pl.BlockSpec(memory_space=pl.ANY)]),
        [],
        (shape_of((3, rows, width), BF16), shape_of((8, width), F32)),
        (
            pl.BlockSpec((3, span, GROUP * 2 * DHEAD), lambda p, *_: (0, which, p)),
            pl.BlockSpec((8, GROUP * 2 * DHEAD), lambda p, *_: (0, p)),
        ),
        [pltpu.VMEM((2, span, 2 * DHEAD), BF16)],
        10 * span * span * width * 2,
        "attend_back",
        exps=span * span * HEADS,
        aliases={} if steps is None else {6: 0},
    )


def project_out(info, mixed, tokens, vectors, weight):
    rows, width = tokens.shape

    def body(info_ref, ins, held, rest):
        mixed_ref, tokens_ref, vector_ref = ins
        normed_ref, low_ref, factor_ref, matrix, sem = rest

        @pl.when(pl.program_id(0) == 0)
        def _():
            start_load(weight, held[0], matrix, info_ref[0], sem)
            wait_load(matrix, sem)

        for part, product in ahead_of(lambda b: dot(mixed_ref[b, :], matrix[...]), 2 * TALL, 2 * SUB):
            branch = product + vector_ref[2:3, :]
            normed, factor = normalize(tokens_ref[part, :].astype(F32) + branch)
            normed_ref[part, :] = normed.astype(BF16)
            low_ref[part, :] = (normed * vector_ref[3:4, :] + vector_ref[4:5, :]).astype(BF16)
            factor_ref[part, :] = jnp.broadcast_to(factor, (2 * SUB, 128))

    return call(
        body,
        (rows // (2 * TALL),),
        info,
        (mixed, tokens, vectors),
        (by_rows(width, 2 * TALL), by_rows(width, 2 * TALL), whole(vectors.shape)),
        [weight],
        (shape_of((rows, width), BF16), shape_of((rows, width), BF16), shape_of((rows, 128), F32)),
        (by_rows(width, 2 * TALL), by_rows(width, 2 * TALL), by_rows(128, 2 * TALL)),
        [pltpu.VMEM((width, width), BF16), pltpu.SemaphoreType.DMA],
        2 * rows * width * width,
        "project_out",
    )


def gelu_both(hidden):
    share = 0.5 * lax.erf(hidden * 0.7071067811865476) + 0.5
    bell = jnp.exp(-0.5 * (hidden * hidden))
    return hidden * share, share + hidden * (bell * 0.3989422804014327)


def feed_in(info, low, bias, weights, begin, end, before):
    rows, width = low.shape
    part = weights[0].columns
    wide = len(weights) * part
    steps = end - begin
    half = part // 2

    def body(info_ref, ins, held, rest):
        low_ref, bias_ref = ins[:2]
        active_ref, slope_ref, matrix, sem = rest
        step = pl.program_id(0)

        @pl.when(step == 0)
        def _():
            start_load(weights[begin], held[0], matrix.at[0], info_ref[0], sem.at[0])

        for i in range(steps):

            @pl.when(step == 2 * i)
            def _():
                wait_load(matrix.at[i], sem.at[i])

        for i in range(1, steps):

            @pl.when(step == 2 * i - 2)
            def _():
                start_load(weights[begin + i], held[i], matrix.at[i], info_ref[0], sem.at[i])

        columns = pl.ds(pl.multiple_of((step % 2) * half, half), half)

        def product_of(some):
            return dot(low_ref[some, :], matrix[step // 2, :, columns])

        for some, product in ahead_of(product_of, rows, FI):
            active, slope = gelu_both(product + bias_ref[...])
            active_ref[some, :] = active.astype(BF16)
            slope_ref[some, :] = slope.astype(BF16)

    columns = pl.BlockSpec((rows, half), lambda i, *_: (0, 2 * begin + i))
    return call(
        body,
        (2 * steps,),
        info,
        (low, bias) + before,
        (whole(low.shape), pl.BlockSpec((1, half), lambda i, *_: (0, 2 * begin + i)))
        + (pl.BlockSpec(memory_space=pl.ANY),) * len(before),
        weights[begin:end],
        (shape_of((rows, wide), BF16), shape_of((rows, wide), BF16)),
        (columns, columns),
        [pltpu.VMEM((steps, width, part), BF16), pltpu.SemaphoreType.DMA((steps,))],
        2 * rows * width * part * steps,
        "feed_in",
        exps=rows * part * steps,
        aliases={3: 0, 4: 1} if before else {},
    )


def feed_out(info, active, normed, cotangent, vectors, weight, span):
    rows, wide = active.shape
    width = weight.columns
    chunks = chunks_of(weight)
    high = wide // chunks

    def body(info_ref, ins, held, rest):
        active_ref, normed_ref, cotangent_ref, vector_ref = ins
        out_ref, branch_ref, sums_ref, matrix, sem = rest
        step = pl.program_id(0)

        @pl.when(step == 0)
        def _():
            start_load(weight, held[0], matrix, info_ref[0], sem, chunks=chunks)
            sums_ref[...] = jnp.zeros_like(sums_ref)

        total = 0.0
        for i in range(chunks):
            some = slice(i * high, (i + 1) * high)

            @pl.when(step == 0)
            def _():
                wait_load(matrix.at[some], sem.at[i])

            total += dot(active_ref[:, some], matrix[some, :])
        sequence = (step * TALL) // span
        length = info_ref[1 + sequence]
        for part in sub_blocks(TALL):
            middle = normed_ref[part, :].astype(F32) * vector_ref[3:4, :] + vector_ref[4:5, :]
            branch = total[part, :] + vector_ref[5:6, :]
            second, factor = normalize(middle + branch)
            gain = vector_ref[6:7, :]
            out_ref[part, :] = (second * gain + vector_ref[7:8, :]).astype(BF16)
            places = step * TALL + part.start + lax.broadcasted_iota(jnp.int32, (SUB, 1), 0)
            valid = places - sequence * span < length
            grad = jnp.where(valid, cotangent_ref[part, :].astype(F32), 0.0)
            sums_ref[0:1, :] += jnp.sum(grad * second, axis=0, keepdims=True)
            sums_ref[1:2, :] += jnp.sum(grad, axis=0, keepdims=True)
            back = norm_back(grad * gain, second, factor)
            branch = back.astype(BF16)
            branch_ref[part, :] = branch
            sums_ref[2:3, :] += jnp.sum(branch.astype(F32), axis=0, keepdims=True)

    return call(
        body,
        (rows // TALL,),
        info,
        (active, normed, cotangent, vectors),
        (by_rows(wide, TALL), by_rows(width, TALL), by_rows(width, TALL), whole(vectors.shape)),
        [weight],
        (
            shape_of((rows, width), BF16),
            shape_of((rows, width), BF16),
            shape_of((8, width), F32),
        ),
        (by_rows(width, TALL), by_rows(width, TALL), whole((8, width))),
        [pltpu.VMEM((wide, width), BF16), pltpu.SemaphoreType.DMA((chunks,))],
        2 * rows * width * wide,
        "feed_out",
    )


def hidden_back(info, branch, slope, outer):
    rows, width = branch.shape
    wide = slope.shape[1]
    steps = chunks_of(outer)
    part = wide // steps

    def body(info_ref, ins, held, rest):
        branch_ref, slope_ref = ins
        hidden_ref, bias_ref, big, sem = rest
        step = pl.program_id(0)

        @pl.when(step == 0)
        def _():
            start_load(outer, held[0], big, info_ref[0], sem, chunks=steps)

        some = pl.ds(pl.multiple_of(step * part, part), part)
        wait_load(big.at[some], sem.at[step])
        total = jnp.zeros((8, part), F32)
        for here, product in ahead_of(lambda b: dot_nt(branch_ref[b, :], big[some, :]), rows, HB):
            grad = (product * slope_ref[here, :].astype(F32)).astype(BF16)
            hidden_ref[here, :] = grad
            total += jnp.sum(grad.astype(F32).reshape(HB // 8, 8, part), axis=0)
        bias_ref[...] = jnp.broadcast_to(jnp.sum(total, axis=0, keepdims=True), bias_ref.shape)

    columns = pl.BlockSpec((rows, part), lambda i, *_: (0, i))
    return call(
        body,
        (steps,),
        info,
        (branch, slope),
        (whole(branch.shape), columns),
        [outer],
        (shape_of((rows, wide), BF16), shape_of((8, wide), F32)),
        (columns, pl.BlockSpec((8, part), lambda i, *_: (0, i))),
        [pltpu.VMEM((wide, width), BF16), pltpu.SemaphoreType.DMA((steps,))],
        2 * rows * width * wide,
        "hidden_back",
    )


def middle_back(info, branch, hidden, normed, factor, vectors, inner, attn):
    rows, width = branch.shape
    wide = hidden.shape[1]
    chunks, part = len(inner), inner[0].columns

    def body(info_ref, ins, held, rest):
        branch_ref, hidden_ref, normed_ref, factor_ref, vector_ref = ins
        proj_ref, mixed_ref, sums_ref, big, small, sem = rest
        step = pl.program_id(0)

        @pl.when(step == 0)
        def _():
            for i in range(chunks):
                start_load(inner[i], held[i], big.at[i], info_ref[0], sem.at[i])
            start_load(attn, held[chunks], small, info_ref[0], sem.at[chunks])
            sums_ref[...] = jnp.zeros_like(sums_ref)

        middle = branch_ref[...].astype(F32)
        for i in range(chunks):

            @pl.when(step == 0)
            def _():
                wait_load(big.at[i], sem.at[i])

            middle += dot_nt(hidden_ref[:, i * part : (i + 1) * part], big[i])

        @pl.when(step == 0)
        def _():
            wait_load(small, sem.at[chunks])

        normed = normed_ref[...].astype(F32)
        sums_ref[0:1, :] += jnp.sum(middle * normed, axis=0, keepdims=True)
        sums_ref[1:2, :] += jnp.sum(middle, axis=0, keepdims=True)
        first = norm_back(middle * vector_ref[3:4, :], normed, factor_ref[:, 0:1])
        proj = first.astype(BF16)
        proj_ref[...] = proj
        sums_ref[2:3, :] += jnp.sum(proj.astype(F32), axis=0, keepdims=True)
        mixed_ref[...] = dot_nt(proj, small[...]).astype(BF16)

    return call(
        body,
        (rows // BLOCK,),
        info,
        (branch, hidden, normed, factor, vectors),
        (by_rows(width), by_rows(wide), by_rows(width), by_rows(128), whole(vectors.shape)),
        inner + [attn],
        (shape_of((rows, width), BF16), shape_of((rows, width), BF16), shape_of((8, width), F32)),
        (by_rows(width), by_rows(width), whole((8, width))),
        [
            pltpu.VMEM((chunks, width, part), BF16),
            pltpu.VMEM((width, width), BF16),
            pltpu.SemaphoreType.DMA((chunks + 1,)),
        ],
        2 * rows * width * wide + 2 * rows * width * width,
        "middle_back",
    )


def input_back(info, proj, steps, weights):
    rows, width = proj.shape

    def body(info_ref, ins, held, rest):
        proj_ref, step_ref = ins
        out_ref, matrix, sem = rest

        @pl.when(pl.program_id(0) == 0)
        def _():
            for i, weight in enumerate(weights):
                start_load(weight, held[i], matrix.at[i], info_ref[0], sem.at[i])

        total = proj_ref[...].astype(F32)
        for i in range(3):

            @pl.when(pl.program_id(0) == 0)
            def _():
                wait_load(matrix.at[i], sem.at[i])

            total += dot_nt(step_ref[i], matrix[i])
        out_ref[...] = total.astype(BF16)

    return call(
        body,
        (rows // BLOCK,),
        info,
        (proj, steps),
        (by_rows(width), pl.BlockSpec((3, BLOCK, width), lambda i, *_: (0, i, 0))),
        weights,
        shape_of((rows, width), BF16),
        by_rows(width),
        [pltpu.VMEM((3, width, width), BF16), pltpu.SemaphoreType.DMA((3,))],
        6 * rows * width * width,
        "input_back",
    )


def weight_grad(info, lefts, rights, places, name):
    rows, height = lefts[0].shape
    slot = height // (8 * places)
    block = 8 * slot
    part = min(1024, rights[0].shape[-1])
    counts = [r.shape[0] if r.ndim == 3 else r.shape[1] // part for r in rights]
    firsts = [sum(counts[:i]) for i in range(len(counts))]
    parts = sum(counts)
    half = height // 2

    def body(info_ref, ins, held, rest):
        left_refs, right_refs = ins[: len(lefts)], ins[len(lefts) :]
        keep_ref, send_ref, sorted_ref = rest
        here = info_ref[0]
        step = pl.program_id(0)
        for left_ref, right_ref, first, count in zip(left_refs, right_refs, firsts, counts):

            @pl.when(step == first)
            def _():
                for z in range(places):
                    turned = left_ref[:, z * block : (z + 1) * block].T
                    for k in range(8):
                        relative = (z * 8 + k) ^ here
                        spot = (relative & 1) * 4 + ((relative >> 1) & 3)
                        spot = spot * places + (relative >> 3)
                        sorted_ref[pl.ds(pl.multiple_of(spot * slot, slot), slot), :] = turned[
                            k * slot : (k + 1) * slot
                        ]

            @pl.when((step >= first) & (step < first + count))
            def _():
                right = right_ref[0] if len(right_ref.shape) == 3 else right_ref[...]
                for out_ref, start in ((keep_ref, 0), (send_ref, half)):
                    for side in range(4):
                        size = half // 4
                        total = dot(sorted_ref[start + side * size : start + (side + 1) * size, :], right)
                        out_ref[side] = total.astype(BF16).reshape(places, slot, part)

    def right_spec(right, first, count):
        place = lambda w: jnp.clip(w - first, 0, count - 1)
        if right.ndim == 3:
            return pl.BlockSpec((1, rows, part), lambda w, *_: (place(w), 0, 0))
        return pl.BlockSpec((rows, part), lambda w, *_: (0, place(w)))

    out = shape_of((4, places, parts * slot, part), BF16)
    out_block = pl.BlockSpec((4, places, slot, part), lambda w, *_: (0, 0, w, 0))
    return call(
        body,
        (parts,),
        info,
        tuple(lefts) + tuple(rights),
        [whole(left.shape) for left in lefts]
        + [right_spec(r, f, c) for r, f, c in zip(rights, firsts, counts)],
        [],
        (out, out),
        (out_block, out_block),
        [pltpu.VMEM((height, rows), BF16)],
        2 * rows * height * parts * part,
        name,
    )


def weight_grad_tall(info, left, right, places, name):
    rows, height = left.shape
    width = right.shape[1]
    slot = height // (8 * places)

    def body(info_ref, ins, held, rest):
        left_ref, right_ref = ins
        keep_ref, send_ref = rest
        here = info_ref[0]
        for side in range(4):
            for out_ref, other in ((keep_ref, 0), (send_ref, 1)):
                which = (here & 7) ^ (2 * side + other)
                some = pl.ds(pl.multiple_of(which * slot, slot), slot)
                out_ref[side, 0] = dot_tn(left_ref[:, some], right_ref[...]).astype(BF16)

    out = shape_of((4, places, slot, width), BF16)
    block = pl.BlockSpec((4, 1, slot, width), lambda z, *_: (0, z, 0, 0))
    return call(
        body,
        (places,),
        info,
        (left, right),
        (
            pl.BlockSpec((rows, 8 * slot), lambda z, info: (0, z ^ (info[0] >> 3))),
            whole(right.shape),
        ),
        [],
        (out, out),
        (block, block),
        [],
        2 * rows * height * width,
        name,
    )


def sums_of(second, first, attn, wide):
    attn = sum(attn)[:2]
    return jnp.concatenate([second[:3], first[:3], attn, wide[:1].reshape(-1, second.shape[1])])


def per_device(
    tokens,
    lengths,
    cotangent,
    query_weight,
    query_bias,
    key_weight,
    value_weight,
    value_bias,
    attn_weight,
    attn_bias,
    first_gain,
    first_shift,
    inner_weight,
    inner_bias,
    outer_weight,
    outer_bias,
    second_gain,
    second_shift,
):
    n = lax.axis_size("fsdp")
    here = lax.axis_index("fsdp").astype(jnp.int32)
    seqs = lengths.shape[0]
    rows, width = tokens.shape
    wide = inner_weight.shape[1]
    span = rows // seqs
    own = query_weight.shape[0]
    tall = outer_weight.shape[0]
    staged = n in (16, 32) and own % 16 == 0
    info = jnp.concatenate([here[None], lengths])

    full = lambda w: lax.all_gather(w, "fsdp", axis=0, tiled=True)
    whole_weight = lambda w: Weight((w,), 0, 0, w.shape[0] // n, w.shape[0], w.shape[1])

    small = jnp.stack(
        (
            query_bias,
            value_bias,
            attn_bias,
            first_gain,
            first_shift,
            outer_bias,
            second_gain,
            second_shift,
        )
    )
    table = jnp.zeros((8 + wide // width, width), BF16)
    table = lax.dynamic_update_slice(table, small, (0, here * own))
    spot = here * tall
    table = lax.dynamic_update_slice(table, inner_bias[None], (8 + spot // width, spot % width))

    if staged:
        places = n // 8
        one = stacked([query_weight, key_weight, value_weight], width)
        two = stacked([inner_weight, attn_weight], width)
        others = gather_line(one)
        for bits in (1, 2, 4):
            table = sum_round(table, (bits,))
        table, two, *others = hold(table, two, *others)
        line = jnp.concatenate([one, *others])
        beside, above = gather_sides(line)
        cut = 3 * own
        others_top = gather_line(two[:cut])
        line, beside, above, two, *others_top = hold(line, beside, above, two, *others_top)
        others_low = gather_line(two[cut:])
        near = (line, beside, above) + gather_across(beside, above)
        table, two, *near = hold(table, two, *near, *others_low)
        near, others_low = near[:5], near[5:]
        table = sum_round(table, [8 * k for k in range(1, places)])
        pieces = near + [flip(piece, 1) for piece in near]
        line_two = jnp.concatenate([two] + [p for pair in zip(others_top, others_low) for p in pair])
        table, line_two, three, *pieces = hold(table, line_two, outer_weight, *pieces)
        qkv_weights = [Weight(pieces, 3 * own, i * own, own, width, width) for i in range(3)]
    else:
        table = sum_everywhere(table)
        qkv_weights = [whole_weight(full(w)) for w in (query_weight, key_weight, value_weight)]
        outer = whole_weight(full(outer_weight))
    table = table.astype(F32)
    vectors, wide_bias = table[:8], table[8:].reshape(1, wide)
    biases = jnp.stack([vectors[0:1], jnp.zeros((1, width), F32), vectors[1:2]])

    blocks = wide // width
    if staged:
        beside, above = gather_sides(line_two)
        others_three = gather_line(three)
        qkv = project_qkv(info, tokens, biases, qkv_weights)
        result = attend(info, qkv, seqs, 0, ())
        beside, above, *result = hold(beside, above, *others_three, *result)
        others_three, result = result[: places - 1], result[places - 1 :]
        near = (line_two, beside, above) + gather_across(beside, above)
        far = tuple(flip(piece, 1) for piece in near[:3])
        line_three = jnp.concatenate([three, *others_three])
        for which in range(1, seqs):
            result = attend(info, qkv, seqs, which, tuple(result))
        mixed, logsum, line_three, *pieces = hold(*result, line_three, *near, *far)
        beside, above = gather_sides(line_three)
        pieces = pieces + [flip(piece, 1) for piece in pieces[3:5]]
        inner = [Weight(pieces, 5 * own, i * own, own, width, width) for i in range(blocks)]
        attn = Weight(pieces, 5 * own, blocks * own, own, width, width)
        normed, low, factor = project_out(info, mixed, tokens, vectors, attn)
        active, slope = feed_in(info, low, wide_bias, inner, 0, blocks // 2, ())
        line_three, beside, above, active, slope = hold(line_three, beside, above, active, slope)
        near = (line_three, beside, above) + gather_across(beside, above)
        far = tuple(flip(piece, 1) for piece in near[:3])
        active, slope = feed_in(info, low, wide_bias, inner, blocks // 2, blocks, (active, slope))
        active, *pieces = hold(active, *near, *far)
        pieces = pieces + [flip(piece, 1) for piece in pieces[3:5]]
        outer = Weight(pieces, tall, 0, tall, wide, width)
    else:
        attn, inner = whole_weight(full(attn_weight)), full(inner_weight)
        inner = [Weight((inner,), 0, 0, own, width, width, i * width) for i in range(blocks)]
        qkv = project_qkv(info, tokens, biases, qkv_weights)
        result = ()
        for which in range(seqs):
            result = attend(info, qkv, seqs, which, tuple(result))
        mixed, logsum = result
        normed, low, factor = project_out(info, mixed, tokens, vectors, attn)
        active, slope = feed_in(info, low, wide_bias, inner, 0, blocks, ())
    output, branch, sums_second = feed_out(
        info, active, normed, cotangent, vectors, outer, span
    )

    def back_of(hidden):
        return middle_back(info, branch, hidden, normed, factor, vectors, inner, attn)

    def attend_all(grad_mixed):
        steps, sums = None, []
        for which in range(seqs):
            steps, some = attend_back(info, qkv, grad_mixed, logsum, seqs, which, steps)
            sums.append(some)
        return steps, sums

    if staged:
        keep_o, send_o = weight_grad_tall(info, active, branch, places, "grad_outer")
        keep_o, send_o, branch = hold(keep_o, send_o, branch)
        got_o = flip(send_o, 1)
        grad_hidden, sums_wide = hidden_back(info, branch, slope, outer)
        got_o, grad_hidden, sums_wide = hold(got_o, grad_hidden, sums_wide)
        sides_o = sides_of(keep_o, got_o)
        grad_hidden, *sides_o = hold(grad_hidden, *sides_o)
        first_o = flip_first(sides_o)
        grad_proj, grad_mixed, sums_first = back_of(grad_hidden)
        first_o, grad_proj, grad_mixed, sums_first = hold(
            first_o, grad_proj, grad_mixed, sums_first
        )
        second_o = flip_second(sides_o, first_o)
        keep, send = weight_grad(
            info, (low, mixed), (grad_hidden, grad_proj), places, "grad_inner_attn"
        )
        second_o, keep, send, grad_mixed = hold(second_o, keep, send, grad_mixed)
        got = flip(send, 1)
        kept_o, arrived_o = flip_line(keep_o, got_o, first_o, second_o)
        steps, some = attend_back(info, qkv, grad_mixed, logsum, seqs, 0, None)
        sums_attn = [some]
        got, kept_o, arrived_o, steps = hold(got, kept_o, arrived_o, steps)
        sides = sides_of(keep, got)
        steps, *sides = hold(steps, *sides)
        first = flip_first(sides)
        for which in range(1, seqs):
            steps, some = attend_back(info, qkv, grad_mixed, logsum, seqs, which, steps)
            sums_attn.append(some)
        keep_two, send_two = weight_grad(info, (tokens,), (steps,), places, "grad_qkv")
        first, steps, keep_two, send_two, *sums_attn = hold(
            first, steps, keep_two, send_two, *sums_attn
        )
        got_two = flip(send_two, 1)
        sums = sums_of(sums_second, sums_first, sums_attn, sums_wide)
        sums = sum_round(sums, (1,))
        second = flip_second(sides, first)
        input_grad = input_back(info, grad_proj, steps, qkv_weights)
        got_two, sums, second, input_grad = hold(got_two, sums, second, input_grad)
        moved_two = flip_diagonal(keep_two, got_two)
        sums = sum_round(sums, [8 * k for k in range(1, places)])
        sums, keep, *moved_two = hold(sums, keep, *moved_two)
        first_two, second_two = flip_whole(keep_two, got_two, moved_two)
        kept, arrived = flip_line(keep, got, first, second)
        sums, first_two, second_two = hold(sums, first_two, second_two)
        sums = sum_round(sum_round(sums, (2,)), (4,))
        kept_two, arrived_two = flip_line(keep_two, got_two, first_two, second_two)
        sums, kept, arrived, kept_o, arrived_o = hold(sums, kept, arrived, kept_o, arrived_o)
        outer_wgrad = add_low(kept_o, *arrived_o)
        both = add_low(kept, *arrived)
        qkv_wgrad = add_low(kept_two, *arrived_two)
        attn_wgrad = both[wide // width * own :]
        inner_wgrad = both[: wide // width * own].reshape(wide // width, own, width)
        inner_wgrad = inner_wgrad.transpose(1, 0, 2).reshape(own, wide)
    else:
        scatter = lambda g: lax.psum_scatter(g, "fsdp", scatter_dimension=0, tiled=True)
        outer_wgrad = scatter(dot_tn(active, branch))
        grad_hidden, sums_wide = hidden_back(info, branch, slope, outer)
        grad_proj, grad_mixed, sums_first = back_of(grad_hidden)
        steps, sums_attn = attend_all(grad_mixed)
        input_grad = input_back(info, grad_proj, steps, qkv_weights)
        inner_wgrad = scatter(dot_tn(low, grad_hidden))
        attn_wgrad = scatter(dot_tn(mixed, grad_proj))
        qkv_wgrad = jnp.concatenate([scatter(dot_tn(tokens, steps[i])) for i in range(3)])
        sums = sum_everywhere(sums_of(sums_second, sums_first, sums_attn, sums_wide))

    mine = lax.dynamic_slice(sums, (0, here * own), (8, own))
    inner_bgrad = lax.dynamic_slice(sums, (8 + spot // width, spot % width), (1, tall))[0]
    return (
        output,
        input_grad,
        qkv_wgrad[:own],
        mine[6],
        qkv_wgrad[own : 2 * own],
        qkv_wgrad[2 * own :],
        mine[7],
        attn_wgrad,
        mine[5],
        mine[3],
        mine[4],
        inner_wgrad,
        inner_bgrad,
        outer_wgrad,
        mine[2],
        mine[0],
        mine[1],
    )


def solution(mesh):
    rows, vector = P("fsdp", None), P("fsdp")
    return jax.shard_map(
        per_device,
        mesh=mesh,
        in_specs=(
            rows,
            vector,
            rows,
            rows,
            vector,
            rows,
            rows,
            vector,
            rows,
            vector,
            vector,
            vector,
            rows,
            vector,
            rows,
            vector,
            vector,
            vector,
        ),
        out_specs=(
            rows,
            rows,
            rows,
            vector,
            rows,
            rows,
            vector,
            rows,
            vector,
            vector,
            vector,
            rows,
            vector,
            rows,
            vector,
            vector,
            vector,
        ),
        check_vma=False,
    )
```
